32 devices in a mesh: section: 2 (over core), tensor: 4 (over z), dp: 4 (over y, x).
Axes of the slice: x: 2, y: 2, z: 4, core: 2. Of those that a mesh axis runs over, the one named last changes fastest.
Arguments:
- layer_input: bfloat16 [2, 1024, 1024], P(None, 'dp'), may hold values from -6 to 6
- out_cotangent: bfloat16 [2, 1024, 1024], P(None, 'dp'), may hold values from -6 to 6
- seq_lengths: int32 [2, 3], replicated, may hold values from 64 to 768, as said below
- norm_gain: float32 [2, 1024], P('section'), may hold values from 0.25 to 1.75
- norm_bias: float32 [2, 1024], P('section'), may hold values from -1.5 to 1.5
- wide_weight: bfloat16 [2, 1024, 3072], P('section', None, 'tensor'), may hold values from -0.1875 to 0.1875
- wide_bias: float32 [2, 3072], P('section', 'tensor'), may hold values from -2.5 to 2.5
- narrow_weight: bfloat16 [2, 1024, 512], P('section', None, 'tensor'), may hold values from -0.1875 to 0.1875
- narrow_bias: float32 [2, 512], P('section', 'tensor'), may hold values from -2.5 to 2.5
- ssm_decay: float32 [2, 512, 64], P('section', 'tensor'), may hold values from 1.953125e-05 to 0.03
- ssm_input: float32 [2, 512, 64], P('section', 'tensor'), may hold values from -4 to 4
- ssm_output: float32 [2, 512, 64], P('section', 'tensor'), may hold values from -0.75 to 0.75
- ssm_skip: float32 [2, 512], P('section', 'tensor'), may hold values from -4 to 4
- lift_weight: bfloat16 [2, 512, 3072], P('section', None, 'tensor'), may hold values from -0.25 to 0.25
- lift_bias: float32 [2, 3072], P('section', 'tensor'), may hold values from -2.5 to 2.5
- down_weight: bfloat16 [2, 3072, 1024], P('section', 'tensor'), may hold values from -0.21875 to 0.21875
- down_bias: float32 [2, 1024], P('section'), may hold values from -2.5 to 2.5
Outputs:
- section_output: float32 [2, 2, 1024, 1024], P('section', None, 'dp', 'tensor')
- input_grad: float32 [2, 2, 1024, 1024], P('section', None, 'dp', 'tensor')
- grad_norm_gain: float32 [2, 1024], P('section', ('tensor', 'dp'))
- grad_norm_bias: float32 [2, 1024], P('section', ('tensor', 'dp'))
- grad_wide_weight: float32 [2, 1024, 3072], P('section', 'dp', 'tensor')
- grad_wide_bias: float32 [2, 3072], P('section', ('tensor', 'dp'))
- grad_narrow_weight: float32 [2, 1024, 512], P('section', 'dp', 'tensor')
- grad_narrow_bias: float32 [2, 512], P('section', ('tensor', 'dp'))
- grad_ssm_decay: float32 [2, 512, 64], P('section', ('tensor', 'dp'))
- grad_ssm_input: float32 [2, 512, 64], P('section', ('tensor', 'dp'))
- grad_ssm_output: float32 [2, 512, 64], P('section', ('tensor', 'dp'))
- grad_ssm_skip: float32 [2, 512], P('section', ('tensor', 'dp'))
- grad_lift_weight: float32 [2, 512, 3072], P('section', 'dp', 'tensor')
- grad_lift_bias: float32 [2, 3072], P('section', ('tensor', 'dp'))
- grad_down_weight: float32 [2, 3072, 1024], P('section', ('tensor', 'dp'))
- grad_down_bias: float32 [2, 1024], P('section', 'dp')
The draws below stay inside these ranges and needn't reach their ends.
Inputs may be any that keep to these rules, and one draw needn't show every extreme that they name: `seq_lengths`: each row holds 3 lengths that add up to 1024; the second is 768, the first and the last add up to 256.
All inputs are finite; a program needn't handle non-finite values.
Results may differ from the reference program's by a relative error of at most 0.015.
Values may be sent and summed in bfloat16 or wider, within the bound.
No kernel may reach another device: no remote copies, remote signals or barrier semaphores. Data moves between devices by JAX's collectives and lax.ppermute only.
A program may use at most 256 MiB of HBM per device.

```python
import math
from functools import partial
import jax
import jax.numpy as jnp
from jax import lax

D = 1024
FF = 3072
H = 512
N = 64
SHARD_TOK = 256
MB = 2
TOKENS_MB = 1024
LAYERS = 2


def draw_seq_lengths(key, part):
    key = jax.random.fold_in(key, 11)
    head_part = jax.random.randint(key, (MB,), SHARD_TOK // 4, SHARD_TOK - SHARD_TOK // 4 + 1)
    longest = jnp.full((MB,), TOKENS_MB - SHARD_TOK, jnp.int32)
    tail_part = SHARD_TOK - head_part
    return jnp.stack([head_part, longest, tail_part], axis=1).astype(jnp.int32)


def steps_of(rng, extent, shards, least, top_value):
    level, own = 1.0, jax.random.fold_in(rng, 6)
    for axis_at, blocks in shards:
        draws = jnp.exp(jax.random.uniform(jax.random.fold_in(own, axis_at), (blocks,), jnp.float32, least / len(shards), top_value / len(shards)))
        level = level * jnp.repeat(draws, extent[axis_at] // blocks).reshape([-1 if axis == axis_at else 1 for axis in range(len(extent))])
    return level


def gaussian(rng, shape, scale, reach, shards=(), held_as=jnp.bfloat16):
    result = scale * jax.random.normal(rng, shape, jnp.float32)
    if shards:
        result = result * steps_of(rng, shape, shards, -0.22, 0.18)
    return jnp.clip(result, -reach, reach).astype(held_as)


def setup_inputs(seed: int = 0) -> dict:
    key_of = jax.random.split(jax.random.key(seed), 18)
    layer_input = gaussian(key_of[0], (MB, TOKENS_MB, D), 1.0, 6.0, ((1, 4),))
    out_cotangent = gaussian(key_of[1], (MB, TOKENS_MB, D), 1.0, 6.0, ((1, 4),))
    seq_lengths = draw_seq_lengths(jax.random.fold_in(key_of[17], 71), 0)
    norm_gain = jnp.clip(1.0 + 0.15 * jax.random.normal(key_of[3], (LAYERS, D), jnp.float32), 0.25, 1.75)
    norm_bias = gaussian(key_of[4], (LAYERS, D), 0.3, 1.5, ((0, 2),), jnp.float32)
    wide_weight = gaussian(key_of[5], (LAYERS, D, FF), D ** -0.5, 0.1875, ((0, 2), (2, 4)))
    wide_bias = gaussian(key_of[6], (LAYERS, FF), 0.5, 2.5, ((0, 2), (1, 4)), jnp.float32)
    narrow_weight = gaussian(key_of[7], (LAYERS, D, H), D ** -0.5, 0.1875, ((0, 2), (2, 4)))
    narrow_bias = gaussian(key_of[8], (LAYERS, H), 0.5, 2.5, ((0, 2), (1, 4)), jnp.float32)
    ssm_decay = jnp.clip(jnp.exp(math.log(0.03) - 7.336937 * jax.random.uniform(key_of[9], (LAYERS, H, N), jnp.float32) ** steps_of(key_of[9], (LAYERS, H, N), ((0, 2), (1, 4)), -0.2, 0.2)), 1.9531249563442543e-05, 0.03)
    ssm_input = gaussian(key_of[10], (LAYERS, H, N), 1.0, 4.0, ((0, 2), (1, 4)), jnp.float32)
    ssm_output = gaussian(key_of[11], (LAYERS, H, N), N ** -0.5, 0.75, ((0, 2), (1, 4)), jnp.float32)
    ssm_skip = gaussian(key_of[12], (LAYERS, H), 1.0, 4.0, ((0, 2), (1, 4)), jnp.float32)
    lift_weight = gaussian(key_of[13], (LAYERS, H, FF), H ** -0.5, 0.25, ((0, 2), (2, 4)))
    lift_bias = gaussian(key_of[14], (LAYERS, FF), 0.5, 2.5, ((0, 2), (1, 4)), jnp.float32)
    down_weight = gaussian(key_of[15], (LAYERS, FF, D), (FF // 4) ** -0.5, 0.21875, ((0, 2), (1, 4)))
    down_bias = gaussian(key_of[16], (LAYERS, D), 0.5, 2.5, ((0, 2),), jnp.float32)
    return {"layer_input": layer_input, "out_cotangent": out_cotangent, "seq_lengths": seq_lengths, "norm_gain": norm_gain, "norm_bias": norm_bias, "wide_weight": wide_weight, "wide_bias": wide_bias, "narrow_weight": narrow_weight, "narrow_bias": narrow_bias, "ssm_decay": ssm_decay, "ssm_input": ssm_input, "ssm_output": ssm_output, "ssm_skip": ssm_skip, "lift_weight": lift_weight, "lift_bias": lift_bias, "down_weight": down_weight, "down_bias": down_bias}


HIGHEST_PRECISION = lax.Precision.HIGHEST
NORM_EPSILON = 1e-05

@jax.custom_vjp
def low(v):
    return lax.optimization_barrier(v.astype(jnp.bfloat16)).astype(jnp.float32)

@jax.custom_vjp
def low_back(v):
    return v

def low_keep(v):
    return (low(v), None)

def low_pass(kept, grad):
    return (grad,)

def back_keep(v):
    return (v, None)

def back_low(kept, grad):
    return (low(grad),)
low.defvjp(low_keep, low_pass)
low_back.defvjp(back_keep, back_low)

def matmul(left, right):
    return jnp.dot(left, right, precision=HIGHEST_PRECISION, preferred_element_type=jnp.float32)

def layer_norm(input_rows, scale, shift_term):
    center = lax.optimization_barrier(jnp.mean(input_rows, axis=-1, keepdims=True))
    offset = input_rows - center
    spread = lax.optimization_barrier(jnp.mean(offset * offset, axis=-1, keepdims=True))
    return offset * lax.rsqrt(spread + NORM_EPSILON) * scale + shift_term

def ssm_block(tables, state, pieces):
    powers, after, kernel, rate_eff, read_out, skip_gain = tables
    input_rows, starts = pieces
    length = input_rows.shape[0]
    counts = jnp.cumsum(starts)
    places = jnp.arange(length)
    spacing = places[:, None] - places[None, :]
    inside = ((spacing >= 0) & (counts[:, None] == counts[None, :])).astype(jnp.float32)
    selector = (spacing[:, :, None] == places[None, None, :]).astype(jnp.float32)
    toeplitz = jnp.einsum('tsk,kc->tsc', selector, kernel, precision=HIGHEST_PRECISION) * inside[:, :, None]
    alive = (counts == 0).astype(jnp.float32)
    tail = (counts == counts[length - 1]).astype(jnp.float32)
    outputs = jnp.einsum('tsc,sc->tc', toeplitz, input_rows, precision=HIGHEST_PRECISION)
    outputs = outputs + alive[:, None] * jnp.einsum('tcn,cn->tc', after, read_out * state, precision=HIGHEST_PRECISION)
    outputs = outputs + skip_gain[None] * input_rows
    fresh = jnp.einsum('scn,sc->cn', powers[::-1], input_rows * tail[:, None], precision=HIGHEST_PRECISION) * rate_eff
    return (fresh + alive[length - 1] * after[length - 1] * state, outputs)

def ssm_sequence(input_rows, starts, decay_rate, rate_input, read_out, skip_gain):
    length = min(128, SHARD_TOK)
    blocks = input_rows.shape[0] // length
    steps = jnp.arange(length).astype(jnp.float32)
    powers = jnp.exp(-steps[:, None, None] * decay_rate[None])
    after = powers * jnp.exp(-decay_rate)[None]
    rate_eff = rate_input * -jnp.expm1(-decay_rate)
    kernel = jnp.einsum('kcn,cn->kc', powers, read_out * rate_eff, precision=HIGHEST_PRECISION)
    stepper = jax.checkpoint(partial(ssm_block, (powers, after, kernel, rate_eff, read_out, skip_gain)))
    state = jnp.zeros(decay_rate.shape, jnp.float32)
    _, outputs = lax.scan(stepper, state, (input_rows.reshape(blocks, length, -1), starts.reshape(blocks, length)))
    return outputs.reshape(input_rows.shape)

def gss_layer(params, input_rows, starts):
    norm_scale, norm_shift, wide_mat, wide_add, narrow_mat, narrow_add, decay_rate, rate_input, read_out, skip_gain, lift_mat, lift_add, down_mat, down_add = params
    normed = low(layer_norm(input_rows, norm_scale, norm_shift))
    wide_act = jax.nn.gelu(low_back(matmul(normed, wide_mat) + wide_add))
    narrow_act = jax.nn.gelu(low_back(matmul(normed, narrow_mat) + narrow_add))
    scanned = low(ssm_sequence(narrow_act, starts, decay_rate, rate_input, read_out, skip_gain))
    lifted = low_back(matmul(scanned, lift_mat) + lift_add)
    gated = low(lifted * wide_act)
    return input_rows + low_back(matmul(gated, down_mat) + down_add)

def reference(layer_input, out_cotangent, seq_lengths, norm_gain, norm_bias, wide_weight, wide_bias, narrow_weight, narrow_bias, ssm_decay, ssm_input, ssm_output, ssm_skip, lift_weight, lift_bias, down_weight, down_bias):
    params = tuple((part.astype(jnp.float32) for part in (norm_gain, norm_bias, wide_weight, wide_bias, narrow_weight, narrow_bias, ssm_decay, ssm_input, ssm_output, ssm_skip, lift_weight, lift_bias, down_weight, down_bias)))
    input_rows = layer_input.astype(jnp.float32)
    cotangent = out_cotangent.astype(jnp.float32)
    begins = jnp.cumsum(seq_lengths, axis=1) - seq_lengths
    position = jnp.arange(TOKENS_MB).astype(jnp.int32)
    starts = lax.optimization_barrier(jnp.sum((position[None, :, None] == begins[:, None, :]).astype(jnp.int32), axis=2))

    def forward(params, input_rows, between):
        first = tuple((part[0] for part in params))
        second = tuple((part[1] for part in params))
        middles = []
        finals = []
        for micro_index in range(MB):
            middle = gss_layer(first, input_rows[micro_index], starts[micro_index]) + between[micro_index]
            middles.append(middle)
            finals.append(gss_layer(second, middle, starts[micro_index]))
        return (jnp.stack(finals), jnp.stack(middles))
    between = jnp.zeros_like(input_rows)
    finals, backward, middles = jax.vjp(forward, params, input_rows, between, has_aux=True)
    grads, grad_inputs, grad_middle = backward(cotangent)
    section_output = jnp.stack([middles, finals])
    input_grad = jnp.stack([grad_inputs, grad_middle])
    return (section_output, input_grad, grads[0], grads[1], grads[2], grads[3], grads[4], grads[5], grads[6], grads[7], grads[8], grads[9], grads[10], grads[11], grads[12], grads[13])
```

```python
from functools import partial

import jax
import jax.numpy as jnp
from jax import lax
from jax.experimental import pallas as pl
from jax.experimental.pallas import tpu as pltpu
from jax.sharding import PartitionSpec as P

F32, BF16 = jnp.float32, jnp.bfloat16
NORM_EPSILON = 1e-05
LANES = 128
GELU_SCALE, GELU_CUBE = 0.7978845608028654, 0.044715
GAIN, SHIFT, DOWN_B, WIDE_B, LIFT_B, NARROW_B, SKIP = 0, 8, 16, 24, 30, 36, 37
MEGA = 1024 * 1024
SPAN = 40_000_000_000
SEGMENTS = 4
IN_VMEM = pl.BlockSpec(memory_space=pltpu.VMEM)
IN_SMEM = pl.BlockSpec(memory_space=pltpu.SMEM)
IN_PLACE = pl.BlockSpec(memory_space=pl.ANY)
IN_HBM = pl.BlockSpec(memory_space=pltpu.HBM)


def mm(left, right):
    return jnp.dot(left, right, preferred_element_type=F32)


def mm_last(left, right):
    return lax.dot_general(left, right, (((1,), (1,)), ((), ())), preferred_element_type=F32)


def mm_first(left, right, precision=None):
    return lax.dot_general(
        left, right, (((0,), (0,)), ((), ())), preferred_element_type=F32, precision=precision
    )


def gelu(z):
    return 0.5 * z * (1.0 + jnp.tanh(GELU_SCALE * (z + GELU_CUBE * z * z * z)))


def gelu_slope(z):
    square = z * z
    bend = jnp.tanh(GELU_SCALE * (z + GELU_CUBE * z * square))
    return 0.5 * (1.0 + bend) + 0.5 * z * (1.0 - bend * bend) * GELU_SCALE * (
        1.0 + 3.0 * GELU_CUBE * square
    )


class Kernel:
    def __init__(self, lengths, length, layer):
        self.lengths, self.length, self.layer = lengths, length, layer

    def __call__(
        self, name, body, outs, vin=(), places=(), picked=(), scratch=(), after=(), spare=6, span=1, keep=False, direct=(), onto=0
    ):
        n_v, n_a, n_p, n_o, n_s = len(vin), len(places), len(picked), len(outs), len(scratch)
        n_w, n_k = len(after), len(picked) if keep else 0
        layer = self.layer

        def run(*refs):
            k = KernelRefs()
            k.meta = placing(refs[0], self.length)
            at = 1
            k.vin = refs[at : at + n_v]
            at += n_v
            k.places = refs[at : at + n_a]
            at += n_a
            pairs = refs[at : at + 2 * n_p]
            at += 2 * n_p + n_w
            k.outs = refs[at : at + n_o]
            at += n_o
            buffers = refs[at : at + n_k]
            at += n_k
            k.scratch = refs[at : at + n_s]
            at += n_s
            if not keep:
                buffers = refs[at : at + n_p]
                at += n_p
            if n_p:
                sems = refs[at]
                mine = k.meta[0] == layer

                def fetch(source):
                    for i in range(n_p):
                        pltpu.make_async_copy(pairs[2 * i + source], buffers[i], sems.at[i]).start()

                pl.when(mine)(partial(fetch, 0))
                pl.when(jnp.logical_not(mine))(partial(fetch, 1))

                def get(i):
                    pltpu.make_async_copy(pairs[2 * i], buffers[i], sems.at[i]).wait()
                    return buffers[i]

                k.get = get
            body(k)

        extra = [] if keep else [pltpu.VMEM(own.shape, own.dtype) for own, _ in picked]
        if n_p:
            extra.append(pltpu.SemaphoreType.DMA((n_p,)))
        held = sum(
            _size(ref.shape) * ref.dtype.itemsize
            for ref in (*scratch, *extra)
            if ref.memory_space == pltpu.VMEM
        )
        flat = [part for pair in picked for part in pair]
        operands = (self.lengths, *vin, *places, *flat, *after)
        return pl.pallas_call(
            run,
            out_shape=[jax.ShapeDtypeStruct(s, d) for s, d in outs]
            + [jax.ShapeDtypeStruct(own.shape, own.dtype) for own, _ in picked[:n_k]],
            in_specs=[IN_SMEM]
            + [IN_VMEM] * n_v
            + [IN_PLACE] * n_a
            + [IN_HBM] * (2 * n_p)
            + [IN_PLACE] * n_w,
            out_specs=[IN_PLACE if i in direct else IN_VMEM for i in range(n_o + n_k)],
            input_output_aliases={1 + n_v + i: i for i in range(onto)},
            scratch_shapes=[*scratch, *extra],
            compiler_params=pltpu.CompilerParams(vmem_limit_bytes=held + spare * MEGA),
            cost_estimate=pl.CostEstimate(flops=span, bytes_accessed=1, transcendentals=0),
            name=name,
        )(*operands)


class KernelRefs:
    pass


def placing(lengths, length):
    section, ti, di = (lax.axis_index(axis) for axis in ("section", "tensor", "dp"))
    first = -di * length
    second = first + lengths[section, 0]
    return [section, ti, di, first, second, second + lengths[section, 1]]


def _size(shape):
    total = 1
    for extent in shape:
        total *= extent
    return total


def vec(pack, first, count):
    column = pack.shape[1] - LANES
    rows = [pack[first + i : first + i + 1, column:] for i in range(count)]
    return rows[0] if count == 1 else jnp.concatenate(rows, axis=1)


def tables(pack):
    return [pack[:, i * LANES : (i + 1) * LANES] for i in range(4)]


def start_in(meta, first, count):
    hit = False
    for i in range(3):
        hit = jnp.logical_or(hit, (meta[3 + i] >= first) & (meta[3 + i] < first + count))
    return hit


def keep_at(meta, place):
    return jnp.where(start_in(meta, place, 1), 0.0, 1.0)


BLOCK = 32


def scan_blocks(meta, length, carry, step, backward=False, block=BLOCK):
    blocks = length // block

    def one(i, carry):
        t0 = pl.multiple_of((blocks - 1 - i if backward else i) * block, block)
        return lax.cond(
            start_in(meta, t0, block),
            lambda c: step(t0, c, True),
            lambda c: step(t0, c, False),
            carry,
        )

    return lax.fori_loop(0, blocks, one, carry)


def row_groups(ref, t0, block, backward=False):
    groups = range(0, block, 8)
    for g in reversed(groups) if backward else groups:
        rows = ref[pl.ds(t0 + g, 8), :]
        for j in reversed(range(8)) if backward else range(8):
            yield g + j, rows[j : j + 1, :]


def end_state(meta, ref, decay, length, backward=False):
    span = length // SEGMENTS
    a = jnp.exp(-decay)

    def step(i, carried, masked):
        out = []
        for g, state in enumerate(carried):
            t0 = pl.multiple_of(g * span + i * 8, 8)
            for j, row in row_groups(ref, t0, 8, backward):
                if backward:
                    state = a * (state + row)
                    if masked:
                        state = state * keep_at(meta, t0 + j)
                else:
                    if masked:
                        state = state * keep_at(meta, t0 + j)
                    state = a * state + row
            out.append(state)
        return tuple(out)

    def one(i, carried):
        i = span // 8 - 1 - i if backward else i
        hit = False
        for g in range(SEGMENTS):
            hit = jnp.logical_or(hit, start_in(meta, g * span + i * 8, 8))
        return lax.cond(hit, lambda c: step(i, c, True), lambda c: step(i, c, False), carried)

    zero = jnp.zeros_like(decay)
    ends = lax.fori_loop(0, span // 8, one, (zero,) * SEGMENTS)
    across = jnp.exp(decay * (-float(span)))
    order = range(SEGMENTS)
    total = zero
    for g in reversed(order) if backward else order:
        through = jnp.where(start_in(meta, g * span, span), 0.0, 1.0)
        total = ends[g] + through * across * total
    return total


def one_minus_exp(d):
    series = 1.0
    for k in range(8, 1, -1):
        series = 1.0 - d * (1.0 / k) * series
    return jnp.where(d < 0.25, d * series, 1.0 - jnp.exp(-d))


def crossing(meta, arrived, decay, length, direction):
    total = jnp.zeros_like(decay)
    for s, part in enumerate(arrived):
        apart = direction * (meta[2] - jnp.bitwise_xor(meta[2], len(arrived) - s)) - 1
        first = -apart * length if direction == 1 else length
        open_way = jnp.logical_and(apart >= 0, jnp.logical_not(start_in(meta, first, apart * length)))
        reach = jnp.exp(decay * (-float(length)) * jnp.maximum(apart, 0).astype(F32))
        total = total + jnp.where(open_way, reach * part[...], 0.0)
    return total


def local(
    layer_input,
    out_cotangent,
    seq_lengths,
    norm_gain,
    norm_bias,
    wide_weight,
    wide_bias,
    narrow_weight,
    narrow_bias,
    ssm_decay,
    ssm_input,
    ssm_output,
    ssm_skip,
    lift_weight,
    lift_bias,
    down_weight,
    down_bias,
):
    section = lax.axis_index("section")
    nt, nd = lax.axis_size("tensor"), lax.axis_size("dp")
    T, D = layer_input.shape[1], layer_input.shape[2]
    FW = wide_weight.shape[2]
    HC = narrow_weight.shape[2]
    H = lift_weight.shape[1]
    N = ssm_decay.shape[2]
    DC = D // nt
    kernels = [Kernel(seq_lengths, T, 0), Kernel(seq_lengths, T, 1)]

    flip = [(0, 1), (1, 0)]

    def swap(x):
        return lax.ppermute(x, "section", flip)

    def make_pack():
        vectors = (
            (norm_gain, GAIN),
            (norm_bias, SHIFT),
            (down_bias, DOWN_B),
            (wide_bias, WIDE_B),
            (lift_bias, LIFT_B),
            (narrow_bias, NARROW_B),
            (ssm_skip, SKIP),
        )
        sources = [ssm_decay, ssm_input, ssm_output]
        sources = [jnp.swapaxes(part, 1, 2)[0] for part in sources]

        def body(k):
            pack, held, sems = k.outs[0], k.scratch[:-1], k.scratch[-1]
            copies = [
                pltpu.make_async_copy(source, target, sems.at[i])
                for i, (source, target) in enumerate(zip(k.places, held))
            ]
            for copy in copies:
                copy.start()
            column = 4 * LANES
            pack[:, column:] = jnp.zeros((N, LANES), F32)
            for copy in copies:
                copy.wait()
            for i, source in zip((0, 2, 3), held):
                pack[:, i * LANES : (i + 1) * LANES] = source[...]
            pack[:, LANES : 2 * LANES] = one_minus_exp(held[0][...])
            for (source, first), ref in zip(vectors, held[3:]):
                for i in range(source.shape[1] // LANES):
                    pack[first + i : first + i + 1, column:] = ref[
                        :, i * LANES : (i + 1) * LANES
                    ]

        places = (*sources, *(v for v, _ in vectors))
        return kernels[0](
            "make_pack",
            body,
            [((N, 5 * LANES), F32)],
            places=places,
            scratch=[pltpu.VMEM(part.shape, F32) for part in places]
            + [pltpu.SemaphoreType.DMA((len(places),))],
            spare=56,
            span=SPAN,
        )[0]

    pack = make_pack()
    pack_other = swap(pack)
    narrow_w = (narrow_weight[0], swap(narrow_weight[0]))
    wide_w = (wide_weight[0], swap(wide_weight[0]))
    lift_w = (lift_weight[0], swap(lift_weight[0]))
    down_w = (down_weight[0], swap(down_weight[0]))

    def paired(part, axis, s):
        n = lax.axis_size(axis)
        return lax.ppermute(part, axis, [(i, i ^ s) for i in range(n)])

    def scatter(parts, axis="tensor"):
        n = len(parts)
        return (parts[0], *(paired(parts[s], axis, n - s) for s in range(1, n)))

    def gather(part, forward=False):
        if forward and nt == 4:
            across = paired(part, "tensor", 2)
            beside = paired(part, "tensor", 1)
            return (part, paired(across, "tensor", 1), across, beside)
        return (part, *(paired(part, "tensor", nt - s) for s in range(1, nt)))

    def paired_parts(meta, keep, give, part):
        for i in range(nt // 2):
            for bit, out in ((0, keep), (1, give)):
                out[i] = part(jnp.bitwise_xor(meta[1], 2 * i + bit)).astype(out.dtype)

    def paired_outs(width):
        return [((nt // 2, T, width), F32), ((nt // 2, T, width), BF16)]

    def parts_join(layer, keep, arrived, after):
        half, width = keep.shape[0] // 2, keep.shape[2]

        def body(k):
            for i in range(2 * half):
                out = k.outs[i % 2]
                out[i // 2] = (k.vin[0][i] + k.vin[1][i].astype(F32)).astype(out.dtype)

        return kernels[layer](
            f"parts_join{layer}",
            body,
            [((half, T, width), F32), ((half, T, width), BF16)],
            vin=(keep, arrived),
            after=after,
        )

    def paired_sum(layer, keep, give, arrived, after):
        step = 2
        while step < nt:
            keep, give = parts_join(layer, keep, arrived, after)
            arrived = paired(give, "tensor", step)
            step *= 2
        return keep, arrived

    def line(value):
        return tuple(paired(value, "dp", nd - 1 - s) for s in range(nd - 1))

    def target(mine, s, n):
        return jnp.bitwise_xor(mine, (n - s) % n)

    HALVES = (FW // 2, FW // 2, D // 2)
    RIGHT = sum(HALVES)

    def turn(layer, sources, after):
        def body(k):
            row = 0
            for source in k.vin:
                for c in range(0, source.shape[1], 256):
                    block = source[:, c : c + 256].astype(F32)
                    k.outs[0][row : row + 256, :] = jnp.transpose(block).astype(BF16)
                    row += 256

        height = sum(part.shape[1] for part in sources)
        return kernels[layer](f"turn{layer}", body, [((height, T), BF16)], vin=sources, after=after)[0]

    def halve(layer, sources, after):
        def body(k):
            at = 0
            for source, width in zip(k.vin, HALVES):
                for out, which in zip(k.outs, (k.meta[0], 1 - k.meta[0])):
                    here = pl.ds(pl.multiple_of(which * width, LANES), width)
                    out[:, at : at + width] = source[:, here]
                at += width

        return kernels[layer](
            f"halve{layer}", body, [((T, RIGHT), BF16)] * 2, vin=sources, after=after
        )

    def choose(layer, pairs, after):
        def body(k):
            for i in range(len(pairs)):
                k.get(i)

        return kernels[layer](f"choose{layer}", body, [], picked=pairs, after=after, keep=True, spare=30)

    def norm_rows(rows, emit):
        def block(i, _):
            here = pl.ds(pl.multiple_of(i * 32, 32), 32)
            x = rows[here, :].astype(F32)
            offset = x - jnp.mean(x, axis=1, keepdims=True)
            spread = jnp.mean(offset * offset, axis=1, keepdims=True)
            inverse = lax.rsqrt(spread + NORM_EPSILON)
            emit(here, offset * inverse, inverse)
            return 0

        lax.fori_loop(0, T // 32, block, 0, unroll=4)

    def norm0(after):
        def body(k):
            xhat, rstd = k.outs
            rows, sems = k.scratch
            copy = pltpu.make_async_copy(k.places[0].at[k.meta[0]], rows, sems.at[0])
            copy.start()
            copy.wait()

            def emit(here, standard, inverse):
                xhat[here, :] = standard
                rstd[here, :] = jnp.broadcast_to(inverse, (32, LANES))

            norm_rows(rows, emit)

        return kernels[0](
            "norm0",
            body,
            [((T, D), F32), ((T, LANES), F32)],
            places=(layer_input,),
            after=after,
            scratch=[pltpu.VMEM((T, D), BF16), pltpu.SemaphoreType.DMA((1,))],
            span=SPAN,
        )

    def front(layer, source, pack, narrow, after=()):
        def body(k):
            meta = k.meta
            normed, narrow_pre, act, final = k.outs[:4]
            if layer == 0:
                pk, upper = k.outs[4:]
                keep_or_give(meta, pk, upper, k.vin[1][...], k.vin[2][...], False)
            else:
                xhat, rstd = k.outs[4:]
                rows = k.scratch[0]
                assemble(meta, k.vin, rows)
                pk, weight = k.vin[nt:]
            gain, shift = vec(pk, GAIN, D // LANES), vec(pk, SHIFT, D // LANES)
            if layer == 0:
                for r in range(0, T, 32):
                    here = slice(r, r + 32)
                    normed[here, :] = (k.vin[0][here, :] * gain + shift).astype(BF16)
                weight = k.get(0)
            else:

                def emit(here, standard, inverse):
                    xhat[here, :] = standard
                    rstd[here, :] = jnp.broadcast_to(inverse, (32, LANES))
                    normed[here, :] = (standard * gain + shift).astype(BF16)

                norm_rows(rows, emit)
            pre = mm(normed[...], weight[...]) + vec(pk, NARROW_B, 1)
            narrow_pre[...] = pre
            act[...] = gelu(pre)
            final[...] = end_state(meta, act, tables(pk)[0], T)

        return kernels[layer](
            f"front{layer}",
            body,
            [((T, D), BF16), ((T, HC), F32), ((T, HC), F32), ((N, HC), F32)]
            + (
                [(pack[0].shape, F32)] * 2
                if layer == 0
                else [((T, D), F32), ((T, LANES), F32)]
            ),
            after=after,
            vin=(source, *pack) if layer == 0 else (*source, pack, narrow),
            picked=(narrow,) if layer == 0 else (),
            keep=True,
            scratch=[] if layer == 0 else [pltpu.VMEM((T, D), BF16)],
            span=SPAN,
        )

    def wide0(normed, pack):
        def body(k):
            bias = vec(k.vin[1], WIDE_B, FW // LANES)
            weight = k.get(0)
            for c in range(0, FW, 256):
                k.outs[0][:, c : c + 256] = (
                    mm(k.vin[0][...], weight[:, c : c + 256]) + bias[:, c : c + 256]
                )

        return kernels[0](
            "wide0",
            body,
            [((T, FW), F32)],
            vin=(normed, pack),
            picked=(wide_w,),
            keep=True,
            spare=6,
        )

    def wide1(normed, d_gated, pack, wide, lift, after):
        def body(k):
            wide_pre, lift_low = k.outs[:2]
            pk, weight, lift = k.vin[2:]
            bias = vec(pk, WIDE_B, FW // LANES)
            for c in range(0, FW, 256):
                pre = mm(k.vin[0][...], weight[:, c : c + 256]) + bias[:, c : c + 256]
                wide_pre[:, c : c + 256] = pre
                lift_low[:, c : c + 256] = (k.vin[1][:, c : c + 256] * gelu(pre)).astype(BF16)
            lift_parts(k.meta, lift_low, lift, k.outs[2:])

        return kernels[1](
            "wide1",
            body,
            [((T, FW), F32), ((T, FW), BF16)] + parted(HC),
            vin=(normed, d_gated, pack, wide, lift),
            after=after,
            span=SPAN,
        )

    def parted(width, rows=T):
        return [((rows, width), F32)] + [((rows, width), BF16)] * (nt - 1)

    def lift_parts(meta, lift_low, lift, sends):
        for s in range(nt):
            at = target(meta[1], s, nt) * HC
            part = mm_last(lift_low[...], lift[pl.ds(pl.multiple_of(at, HC), HC), :])
            sends[s][...] = part.astype(sends[s].dtype)

    def carry(layer, act, arrived, pack, after=()):
        def body(k):
            meta = k.meta
            u = k.vin[0]
            entering, scanned = k.outs
            local_out = k.scratch[0]
            pk = k.vin[1]
            decay, grown, rate_in, read_out = tables(pk)
            skip = vec(pk, SKIP, 1)
            a, read = jnp.exp(-decay), read_out * rate_in * grown
            state = crossing(meta, k.vin[2:], decay, T, 1)
            entering[...] = state

            def step(t0, state, masked):
                outs = []
                for j, row in row_groups(u, t0, BLOCK):
                    if masked:
                        state = state * keep_at(meta, t0 + j)
                    state = a * state + row
                    outs.append(jnp.sum(read * state, axis=0, keepdims=True) + skip * row)
                for g in range(0, BLOCK, 8):
                    local_out[pl.ds(t0 + g, 8), :] = jnp.concatenate(outs[g : g + 8], axis=0)
                return state

            scan_blocks(meta, T, state, step)
            scanned[...] = local_out[...].astype(BF16)

        return kernels[layer](
            f"carry{layer}",
            body,
            [((N, HC), F32), ((T, HC), BF16)],
            vin=(act, pack, *arrived),
            after=after,
            scratch=[pltpu.VMEM((T, HC), F32)],
            span=SPAN,
        )

    def assemble(meta, parts, whole):
        width = parts[0].shape[1]
        for s in range(nt):
            at = target(meta[1], s, nt) * width
            whole[:, pl.ds(pl.multiple_of(at, width), width)] = parts[s][...]

    def down_parts(meta, gated, down, sends):
        for s in range(nt):
            at = target(meta[1], s, nt) * DC
            part = mm(gated[...], down[:, pl.ds(pl.multiple_of(at, DC), DC)])
            sends[s][...] = part.astype(sends[s].dtype)

    def middle0(pieces, wide_pre, pack, lift, down):
        def body(k):
            scanned, lifted, gated = k.outs[:3]
            assemble(k.meta, k.vin[:nt], scanned)
            wide_pre, pk, lift, down = k.vin[nt:]
            bias = vec(pk, LIFT_B, FW // LANES)
            for c in range(0, FW, 256):
                part = mm(scanned[...], lift[:, c : c + 256]) + bias[:, c : c + 256]
                lifted[:, c : c + 256] = part
                gated[:, c : c + 256] = (part * gelu(wide_pre[:, c : c + 256])).astype(BF16)
            down_parts(k.meta, gated, down, k.outs[3:])

        return kernels[0](
            "middle0",
            body,
            [((T, H), BF16), ((T, FW), F32), ((T, FW), BF16)] + parted(DC),
            vin=(*pieces, wide_pre, pack, lift, down),
            span=SPAN,
        )

    def middle1(pieces, wide_pre, d_gated, pack, lift):
        def body(k):
            scanned, gated, wide_low = k.outs
            assemble(k.meta, k.vin[:nt], scanned)
            pre, grad, pk, lift = k.vin[nt:]
            bias = vec(pk, LIFT_B, FW // LANES)
            for c in range(0, FW, 256):
                part = mm(scanned[...], lift[:, c : c + 256]) + bias[:, c : c + 256]
                z = pre[:, c : c + 256]
                gated[:, c : c + 256] = (part * gelu(z)).astype(BF16)
                wide_low[:, c : c + 256] = (grad[:, c : c + 256] * part * gelu_slope(z)).astype(BF16)

        return kernels[1](
            "middle1",
            body,
            [((T, H), BF16), ((T, FW), BF16), ((T, FW), BF16)],
            vin=(*pieces, wide_pre, d_gated, pack, lift),
            span=SPAN,
        )

    def top_parts(gated, down, after):
        def body(k):
            gated, down = k.vin
            paired_parts(
                k.meta,
                *k.outs,
                lambda at: mm(gated[...], down[:, pl.ds(pl.multiple_of(at * DC, DC), DC)]),
            )

        return kernels[1]("top_parts", body, paired_outs(DC), vin=(gated, down), after=after)

    def column_rows(pk, first, at):
        per = DC // LANES
        best = vec(pk, first, per)
        for i in range(1, nt):
            best = jnp.where(at == i, vec(pk, first + i * per, per), best)
        return best

    def keep_or_give(meta, keep, give, first, second, by_layer=True):
        lower = meta[0] == 0
        keep[...] = jnp.where(lower, first, second)
        give[0 : keep.shape[0], :] = jnp.where(lower, second, first).astype(give.dtype)

    def layer_output(layer, before, parts, pack, after=()):
        def body(k):
            meta = k.meta
            if layer == 0:
                rows = k.scratch[0]
                copy = pltpu.make_async_copy(
                    k.places[0].at[meta[0], :, pl.ds(pl.multiple_of(meta[1] * DC, DC), DC)],
                    rows,
                    k.scratch[1].at[0],
                )
                copy.start()
                copy.wait()
                total = rows[...].astype(F32)
            else:
                total = k.vin[-1][...] + k.vin[1][0] + k.vin[2][0].astype(F32)
            for part in k.vin[1 : 1 + nt] if layer == 0 else ():
                total = total + part[...].astype(F32)
            total = total + column_rows(k.vin[0], DOWN_B, meta[1])
            if layer == 0:
                k.outs[0][...] = total
                k.outs[1][...] = total.astype(BF16)
            else:
                keep_or_give(meta, k.outs[0], k.outs[1], k.vin[-1][...], total)

        return kernels[layer](
            f"layer_output{layer}",
            body,
            [((T, DC), F32), ((T, DC), BF16 if layer == 0 else F32)],
            vin=(pack, *parts) if layer == 0 else (pack, *parts, before),
            after=after,
            places=(before,) if layer == 0 else (),
            scratch=[pltpu.VMEM((T, DC), BF16), pltpu.SemaphoreType.DMA((1,))] if layer == 0 else [],
            span=1 if layer else SPAN,
        )

    def grad_gated1(down, after):
        def body(k):
            rows = k.outs[1]
            copy = pltpu.make_async_copy(k.places[0].at[k.meta[0]], rows, k.scratch[0].at[0])
            copy.start()
            copy.wait()
            down = k.vin[0]
            for c in range(0, FW, 256):
                k.outs[0][:, c : c + 256] = mm_last(rows[...], down[c : c + 256, :])

        return kernels[1](
            "grad_gated1",
            body,
            [((T, FW), F32), ((T, D), BF16)],
            places=(out_cotangent,),
            vin=(down,),
            after=after,
            scratch=[pltpu.SemaphoreType.DMA((1,))],
        )

    def grad_middle0(pieces, wide_pre, lifted, down, lift, after=()):
        def body(k):
            wide_low, low, rows = k.outs[:3]
            pre, raised, down, lift = k.vin[nt:]
            assemble(k.meta, k.vin[:nt], rows)
            for c in range(0, FW, 256):
                grad = mm_last(rows[...], down[c : c + 256, :])
                z = pre[:, c : c + 256]
                low[:, c : c + 256] = (grad * gelu(z)).astype(BF16)
                wide_low[:, c : c + 256] = (
                    grad * raised[:, c : c + 256] * gelu_slope(z)
                ).astype(BF16)
            lift_parts(k.meta, low, lift, k.outs[3:])

        return kernels[0](
            "grad_middle0",
            body,
            [((T, FW), BF16), ((T, FW), BF16), ((T, D), BF16)] + parted(HC),
            vin=(*pieces, wide_pre, lifted, down, lift),
            after=after,
            span=SPAN,
        )

    def adjoint_local(layer, parts, pack, after=()):
        def body(k):
            grads, first = k.outs
            total = k.vin[1][...]
            for part in k.vin[2:]:
                total = total + part[...].astype(F32)
            grads[...] = total
            first[...] = end_state(k.meta, grads, tables(k.vin[0])[0], T, backward=True)

        return kernels[layer](
            f"adjoint_local{layer}",
            body,
            [((T, HC), F32), ((N, HC), F32)],
            vin=(pack, *parts),
            after=after,
            span=SPAN,
        )

    def adjoint(layer, d_scanned, narrow_pre, arrived, pack, after=()):
        def body(k):
            meta = k.meta
            grads, pre, pk = k.vin[:3]
            after, narrow_low = k.outs
            d_narrow = k.scratch[0]
            decay, grown, rate_in, read_out = tables(pk)
            skip = vec(pk, SKIP, 1)
            a, read = jnp.exp(-decay), read_out * rate_in * grown
            incoming = crossing(meta, k.vin[3:], decay, T, -1)
            after[...] = incoming

            def step(t0, z, masked):
                outs = [None] * BLOCK
                for j, row in row_groups(grads, t0, BLOCK, True):
                    w = z + row
                    outs[j] = jnp.sum(read * w, axis=0, keepdims=True) + skip * row
                    z = a * w
                    if masked:
                        z = z * keep_at(meta, t0 + j)
                for g in range(0, BLOCK, 8):
                    d_narrow[pl.ds(t0 + g, 8), :] = jnp.concatenate(outs[g : g + 8], axis=0)
                return z

            scan_blocks(meta, T, incoming, step, backward=True)
            narrow_low[...] = (d_narrow[...] * gelu_slope(pre[...])).astype(BF16)

        return kernels[layer](
            f"adjoint{layer}",
            body,
            [((N, HC), F32), ((T, HC), BF16)],
            vin=(d_scanned, narrow_pre, pack, *arrived),
            after=after,
            scratch=[pltpu.VMEM((T, HC), F32)],
            span=SPAN,
        )

    LATE = D // 2 + 2 * N

    def ssm_grads(layer, act, entering, d_scanned, incoming, turned, narrow_low, pack, upper, after):
        def body(k):
            meta = k.meta
            u, enter, grads, incoming, low, pk = k.vin[:6]
            states, lefts, sems = k.scratch[:3]
            late = k.outs[0] if layer == 1 else k.scratch[3]
            copy = pltpu.make_async_copy(k.places[0].at[0:D, :], lefts, sems.at[0])
            copy.start()
            decay, grown, rate_in, read_out = tables(pk)
            a = jnp.exp(-decay)
            zero = jnp.zeros((N, HC), F32)

            def ahead(t0, state, masked):
                for j, row in row_groups(u, t0, BLOCK):
                    if masked:
                        state = state * keep_at(meta, t0 + j)
                    states[t0 + j] = state
                    state = a * state + row
                return state

            scan_blocks(meta, T, enter[...], ahead)

            def back(t0, carried, masked):
                z, with_rows, with_states = carried
                rows = row_groups(u, t0, BLOCK, True)
                for (j, row), (_, grad) in zip(rows, row_groups(grads, t0, BLOCK, True)):
                    w = z + grad
                    with_rows = with_rows + w * row
                    with_states = with_states + w * states[t0 + j]
                    z = a * w
                    if masked:
                        z = z * keep_at(meta, t0 + j)
                return z, with_rows, with_states

            _, with_rows, with_states = scan_blocks(
                meta, T, (incoming[...], zero, zero), back, backward=True
            )
            b = rate_in * grown
            first, second = slice(D // 2, D // 2 + N), slice(D // 2 + N, D // 2 + 2 * N)
            late[first, 0:LANES] = a * read_out * (rate_in * with_rows - b * with_states)
            late[first, LANES:] = grown * read_out * with_rows
            late[second, 0:LANES] = b * with_rows
            late[second, LANES:] = zero
            row = D // 2 + N
            late[row : row + 1, LANES:] = jnp.sum(low[...].astype(F32), axis=0, keepdims=True)
            late[row + 1 : row + 2, LANES:] = jnp.sum(u[...] * grads[...], axis=0, keepdims=True)
            copy.wait()
            for h in range(2):
                late[0 : D // 2, h * LANES : (h + 1) * LANES] = mm(
                    lefts[h * (D // 2) : (h + 1) * (D // 2), :], low[...]
                )
            if layer == 0:
                keep_or_give(meta, k.outs[0], k.outs[1], late[...], k.vin[6][...])

        return kernels[layer](
            f"ssm_grads{layer}",
            body,
            [((LATE, 2 * LANES), F32)] * (2 - layer),
            vin=(act, entering, d_scanned, incoming, narrow_low, pack, *upper),
            places=(turned,),
            span=1 if layer else SPAN,
            after=after,
            scratch=[
                pltpu.VMEM((T, N, HC), F32),
                pltpu.VMEM((D, T), BF16),
                pltpu.SemaphoreType.DMA((1,)),
            ]
            + ([pltpu.VMEM((LATE, 2 * LANES), F32)] if layer == 0 else []),
        )

    def grad_normed(layer, wide_low, narrow_low, xhat, pack, wide, narrow, after=()):
        def body(k):
            meta = k.meta
            wide_low, narrow_in, standard, gains, wide, narrow = k.vin
            ones = jnp.ones((8, DC), BF16)
            sums = jnp.zeros((16, T), F32)
            for s in range(nt):
                at = target(meta[1], s, nt)
                here = pl.ds(pl.multiple_of(at * DC, DC), DC)
                part = mm_last(wide_low[...], wide[here, :]) + mm_last(
                    narrow_in[...], narrow[here, :]
                )
                scaled = part * column_rows(gains, GAIN, at)
                with_x = scaled * standard[:, here]
                sums = sums + jnp.concatenate(
                    [mm_last(ones, scaled.astype(BF16)), mm_last(ones, with_x.astype(BF16))], axis=0
                )
                k.outs[s][0:T, :] = part.astype(k.outs[s].dtype)
            for s in range(nt):
                k.outs[s][T:, :] = sums.astype(k.outs[s].dtype)

        return kernels[layer](
            f"grad_normed{layer}",
            body,
            parted(DC, T + 16),
            vin=(wide_low, narrow_low, xhat, pack, wide, narrow),
            after=after,
            span=SPAN,
        )

    def layer_grad(layer, parts, rstd, xhat, grad_out, pack, after):
        def body(k):
            meta = k.meta
            here = pl.ds(pl.multiple_of(meta[1] * DC, DC), DC)
            standard, sems = k.scratch[0], k.scratch[1]
            copy = pltpu.make_async_copy(k.places[0].at[:, here], standard, sems.at[0])
            copy.start()
            if layer == 1:
                copy_out = pltpu.make_async_copy(
                    k.places[1].at[meta[0], :, here], k.scratch[2], sems.at[1]
                )
                copy_out.start()
            total, sums = k.vin[0][0:T, :], k.vin[0][T:, :]
            for part in k.vin[1:nt]:
                total = total + part[0:T, :].astype(F32)
                sums = sums + part[T:, :].astype(F32)
            inverse = k.vin[nt]
            row = lax.broadcasted_iota(jnp.int32, (16, LANES), 0)
            first = mm_first(sums, (row == 0).astype(F32), lax.Precision.HIGHEST) * (1.0 / D)
            second = mm_first(sums, (row == 8).astype(F32), lax.Precision.HIGHEST) * (1.0 / D)
            scaled = total * column_rows(k.vin[nt + 1], GAIN, meta[1])
            copy.wait()
            if layer == 1:
                copy_out.wait()
                grad_in = k.scratch[2][...].astype(F32)
            else:
                grad_in = k.vin[nt + 2][...]
            if layer == 1:
                result = k.outs[0]
            else:
                keep, give, upper = k.outs[0], k.outs[1], k.vin[nt + 2]
                result = k.scratch[2]
            for c in range(0, DC, LANES):
                x = standard[:, c : c + LANES]
                grad = grad_in[0:T, c : c + LANES] + inverse[...] * (
                    scaled[:, c : c + LANES] - first - x * second
                )
                result[0:T, c : c + LANES] = grad
                if layer == 1:
                    k.outs[1][:, c : c + LANES] = grad.astype(BF16)
            result[T:, :] = jnp.zeros((8, DC), F32)
            result[T : T + 1, :] = jnp.sum(total * standard[...], axis=0, keepdims=True)
            result[T + 1 : T + 2, :] = jnp.sum(total, axis=0, keepdims=True)
            if layer == 0:
                keep_or_give(meta, keep, give, result[...], upper[...])
                give[T + 8 :, :] = jnp.zeros((8, DC), BF16)

        return kernels[layer](
            f"layer_grad{layer}",
            body,
            [((T + 8, DC), F32), ((T, DC), BF16)]
            if layer == 1
            else [((T + 8, DC), F32), ((T + 16, DC), BF16)],
            after=after,
            vin=(*parts, rstd, pack) + (() if layer == 1 else (grad_out,)),
            places=(xhat,) + ((grad_out,) if layer == 1 else ()),
            scratch=[pltpu.VMEM((T, DC), F32), pltpu.SemaphoreType.DMA((2,))]
            + [pltpu.VMEM((T, DC), BF16) if layer == 1 else pltpu.VMEM((T + 8, DC), F32)],
            span=SPAN,
        )

    RW, RL, RD = D // nd, H // nd, FW // nd
    CW, CD = HALVES[0] // LANES, HALVES[2] // LANES
    AT_L = RW * CW
    AT_D = AT_L + RL * CW
    AT_V = AT_D + RD * CD
    BIG = AT_V + 16
    CUT = AT_L + 2 * RL
    STEPS = nd.bit_length() - 1

    def mirrored(s):
        return sum(((s >> b) & 1) << (STEPS - 1 - b) for b in range(STEPS))

    def block_outs(count):
        return [((count, rows, LANES), BF16) for rows in (CUT, BIG - CUT) for _ in range(2)]

    def to_pairs(blocks, step):
        return (
            paired(blocks[1], "dp", 1 << step),
            paired(blocks[3], "dp", 1 << (STEPS - 1 - step)),
        )

    def blocks_join(layer, blocks, arrived, after):
        count = blocks[0].shape[0] // 2

        def body(k):
            for h in range(2):
                for i in range(2 * count):
                    part = k.vin[2 * h][i].astype(F32) + k.vin[2 * h + 1][i].astype(F32)
                    k.outs[2 * h + i % 2][i // 2] = part.astype(BF16)

        return kernels[layer](
            f"blocks_join{layer}",
            body,
            block_outs(count),
            vin=(blocks[0], arrived[0], blocks[2], arrived[1]),
            after=after,
        )

    def put(k, s, row, value):
        first = row < CUT
        i = s if first else mirrored(s)
        out = k.outs[i % 2 if first else 2 + i % 2]
        row -= 0 if first else CUT
        out[i // 2, row : row + value.shape[0], :] = value.astype(BF16)

    def weight_grads(layer, lefts, rights, after):
        def body(k):
            meta = k.meta
            left, right = k.vin[:2], k.vin[2:]

            def product(row, rows, at, width, at_row):
                columns = slice(at, at + width)
                for s in range(nd):
                    first = row + jnp.bitwise_xor(meta[2], s) * rows
                    here = pl.ds(pl.multiple_of(first, 16), rows)
                    part = mm(left[0][here, :], right[0][:, columns])
                    part = part + mm(left[1][here, :], right[1][:, columns])
                    for h in range(0, width, LANES):
                        put(k, s, at_row + h // LANES * rows, part[:, h : h + LANES])

            product(0, RW, 0, HALVES[0], 0)
            product(D, RL, HALVES[0], HALVES[1], AT_L)
            product(D + H, RD, HALVES[0] + HALVES[1], HALVES[2], AT_D)
            sums = k.scratch[0]
            sums[...] = jnp.zeros((16, LANES), F32)
            for i in range(RIGHT // LANES):
                here = slice(i * LANES, (i + 1) * LANES)
                total = jnp.sum(right[0][:, here].astype(F32), axis=0, keepdims=True)
                total = total + jnp.sum(right[1][:, here].astype(F32), axis=0, keepdims=True)
                sums[i : i + 1, :] = total
            for s in range(nd):
                put(k, s, AT_V, sums[...])

        return kernels[layer](
            f"weight_grads{layer}",
            body,
            block_outs(nd // 2),
            vin=(*lefts, *rights),
            after=after,
            scratch=[pltpu.VMEM((16, LANES), F32)],
        )

    SMALL = RW + 3 * N + 16

    def late_join(keep, other, grad, grad_other, after):
        def body(k):
            meta = k.meta
            own, other, grad, grad_other = k.vin
            rest = k.scratch[0]

            def summed(rows, columns):
                return own[rows, columns] + other[rows, columns]

            half = D // 2
            left, right = slice(0, LANES), slice(LANES, 2 * LANES)
            upper = slice(half, half + N)
            rest[0:N, :] = summed(upper, left)
            rest[N : 2 * N, :] = summed(upper, right)
            rest[2 * N : 3 * N, :] = summed(slice(half + N, half + 2 * N), left)
            rest[3 * N : 3 * N + 8, :] = summed(slice(half + N, half + N + 8), right)
            rest[3 * N + 8 :, :] = jnp.zeros((8, LANES), F32)
            per = DC // LANES
            for i in range(2):
                row = grad[T + i : T + i + 1, :] + grad_other[T : T + 16, :].astype(F32)[i : i + 1, :]
                for h in range(per):
                    first = 3 * N + 8 + i * per + h
                    rest[first : first + 1, :] = row[:, h * LANES : (h + 1) * LANES]
            for s in range(nd):
                at = target(meta[2], s, nd) * RW
                here = pl.ds(pl.multiple_of(lax.rem(at, half), 16), RW)
                for h in range(2):

                    def put(h=h, out=k.outs[s]):
                        columns = slice(h * LANES, (h + 1) * LANES)
                        out[0:RW, :] = summed(here, columns).astype(BF16)

                    pl.when(at // half == h)(put)
                k.outs[s][RW:, :] = rest[...].astype(BF16)

        return kernels[0](
            "late_join",
            body,
            [((SMALL, LANES), BF16)] * nd,
            vin=(keep, other, grad, grad_other),
            after=after,
            scratch=[pltpu.VMEM((3 * N + 16, LANES), F32)],
        )

    def pick(meta, flat, out):
        width = out.shape[1]
        best = flat[:, 0:width]
        for i in range(1, nd):
            best = jnp.where(meta[2] == i, flat[:, i * width : (i + 1) * width], best)
        out[...] = best

    def chunk(meta, source, first, count, out):
        flat = [source[first + i : first + i + 1, :] for i in range(count)]
        pick(meta, flat[0] if count == 1 else jnp.concatenate(flat, axis=1), out)

    def big_sum(layer, blocks, arrived, upper, after):
        def body(k):
            for h, (first, rows) in enumerate(((0, CUT), (CUT, BIG - CUT))):
                for r in range(0, rows, 256):
                    inner = slice(r, min(r + 256, rows))
                    here = slice(first + inner.start, first + inner.stop)
                    total = k.vin[2 * h][0, inner, :].astype(F32)
                    total = total + k.vin[2 * h + 1][0, inner, :].astype(F32)
                    if layer == 1:
                        k.outs[0][here, :] = total
                    else:
                        lower = k.meta[0] == 0
                        other = k.vin[4][here, :]
                        k.outs[0][here, :] = jnp.where(lower, total, other)
                        k.outs[1][here, :] = jnp.where(lower, other, total).astype(BF16)

        return kernels[layer](
            f"big_sum{layer}",
            body,
            [((BIG, LANES), F32)] + ([((BIG, LANES), BF16)] if layer == 0 else []),
            vin=(blocks[0], arrived[0], blocks[2], arrived[1], *upper),
            after=after,
        )

    def late_sum(parts):
        def body(k):
            total = k.vin[0][...].astype(F32)
            for part in k.vin[1:]:
                total = total + part[...].astype(F32)
            k.outs[0][...] = total

        return kernels[0]("late_sum", body, [((SMALL, LANES), F32)], vin=parts, span=SPAN)[0]

    def big_places():
        return ((0, RW, CW), (AT_L, RL, CW), (AT_D, RD, CD))

    def own_columns(keep, grad, grad_other, after):
        def body(k):
            meta = k.meta
            *outs, grads = k.outs
            rows, sems = k.scratch
            rows[...] = k.vin[0][0:T, :].astype(F32)
            moves = [(k.places[1].at[0:T, :], grads.at[0, meta[0]]), (rows, grads.at[0, 1 - meta[0]])]
            for out, (first, height, columns) in zip(outs, big_places()):
                for c in range(columns):
                    at = pl.multiple_of((meta[0] * columns + c) * LANES, LANES)
                    moves.append(
                        (
                            k.places[0].at[first + c * height : first + (c + 1) * height, :],
                            out.at[0, :, pl.ds(at, LANES)],
                        )
                    )
            moves = [
                pltpu.make_async_copy(source, out, sems.at[i])
                for i, (source, out) in enumerate(moves)
            ]
            for move in moves:
                move.start()
            for move in moves:
                move.wait()

        return kernels[0](
            "own_columns",
            body,
            [((1, RW, FW), F32), ((1, RL, FW), F32), ((1, RD, D), F32), ((1, 2, T, DC), F32)],
            vin=(grad_other,),
            places=(keep, grad),
            after=after,
            direct=(0, 1, 2, 3),
            scratch=[pltpu.VMEM((T, DC), F32), pltpu.SemaphoreType.DMA((2 + 2 * CW + CD,))],
        )

    def finish(own, big, small, output, output_other):
        def body(k):
            meta = k.meta
            wide, lift, down, rows, turned, sems = k.scratch
            by_wide, by_lift, by_down = k.outs[:3]
            wide_b, lift_b, down_b = k.outs[3:6]
            by_narrow, narrow_b, *by_ssm, by_skip, gain, shift, outputs = k.outs[6:]
            keep, give, late = k.vin
            moves = [
                (k.places[3], outputs.at[0, meta[0]]),
                (k.places[4], outputs.at[0, 1 - meta[0]]),
                (k.places[5].at[0:RW, :], by_narrow.at[0]),
            ]
            moves = [
                pltpu.make_async_copy(source, out, sems.at[3 + i])
                for i, (source, out) in enumerate(moves)
            ]
            for move in moves:
                move.start()
            for q, (buffer, out, (first, height, columns)) in enumerate(
                zip((wide, lift, down), (by_wide, by_lift, by_down), big_places())
            ):
                for c in range(columns):
                    part = give[first + c * height : first + (c + 1) * height, :]
                    buffer[:, c * LANES : (c + 1) * LANES] = part.astype(F32)
                width = columns * LANES
                at = pl.multiple_of((1 - meta[0]) * width, LANES)
                moves.append(
                    pltpu.make_async_copy(buffer, out.at[0, :, pl.ds(at, width)], sems.at[q])
                )
                moves[-1].start()
            lower = meta[0] == 0
            own, other = keep[AT_V:, :], give[AT_V:, :].astype(F32)
            rows[0:16, :] = jnp.where(lower, own, other)
            rows[16:, :] = jnp.where(lower, other, own)
            at = 0
            for columns, out in ((CW, wide_b), (CW, lift_b), (CD, down_b)):
                whole = [rows[h + at + i : h + at + i + 1, :] for h in (0, 16) for i in range(columns)]
                pick(meta, jnp.concatenate(whole, axis=1), out)
                at += columns
            rows[0:16, :] = late[RW + 3 * N :, :]
            chunk(meta, rows, 0, 1, narrow_b)
            chunk(meta, rows, 1, 1, by_skip)
            chunk(meta, rows, 8, DC // LANES, gain)
            chunk(meta, rows, 8 + DC // LANES, DC // LANES, shift)
            per = HC // nd
            for i in range(3):
                turned[...] = jnp.transpose(late[RW + i * N : RW + (i + 1) * N, :])
                by_ssm[i][0] = turned[pl.ds(pl.multiple_of(meta[2] * per, per), per), :]
            for move in moves:
                move.wait()

        return kernels[0](
            "finish",
            body,
            [
                *((part.shape, F32) for part in own),
                ((1, FW // nd), F32),
                ((1, FW // nd), F32),
                ((1, D // nd), F32),
                ((1, RW, HC), F32),
                ((1, HC // nd), F32),
                ((1, HC // nd, N), F32),
                ((1, HC // nd, N), F32),
                ((1, HC // nd, N), F32),
                ((1, HC // nd), F32),
                ((1, DC // nd), F32),
                ((1, DC // nd), F32),
                ((1, 2, T, DC), F32),
            ],
            vin=(*big, small),
            places=(*own, output, output_other, small),
            direct=(0, 1, 2, 6, 14),
            onto=3,
            scratch=[
                pltpu.VMEM((RW, HALVES[0]), F32),
                pltpu.VMEM((RL, HALVES[1]), F32),
                pltpu.VMEM((RD, HALVES[2]), F32),
                pltpu.VMEM((32, LANES), F32),
                pltpu.VMEM((HC, N), F32),
                pltpu.SemaphoreType.DMA((6,)),
            ],
        )

    xhat0, rstd0 = norm0(after=())
    normed0, narrow_pre0, act0, final0, pack0, pack1, narrow_w0 = front(
        0, xhat0, (pack, pack_other), narrow_w
    )
    arrived = line(final0)
    wide_pre0, wide_w0 = wide0(normed0, pack0)
    enter0, scanned0 = carry(0, act0, arrived, pack0, after=(wide_pre0,))
    pieces = gather(scanned0)
    lift_w0, down_w0 = choose(0, (lift_w, down_w), after=(scanned0,))
    scanned_all0, lifted0, gated0, *sends = middle0(pieces, wide_pre0, pack0, lift_w0, down_w0)
    parts = scatter(sends)
    narrow_w1, wide_w1, lift_w1, down_w1 = choose(
        1, (narrow_w, wide_w, lift_w, down_w), after=(sends[0],)
    )
    d_gated1, out_low1 = grad_gated1(down_w1, after=(sends[0],))
    hidden, hidden_low = layer_output(0, layer_input, parts, pack0, after=(d_gated1,))
    pieces = gather(hidden_low, forward=True)
    lefts0 = turn(0, (normed0, scanned_all0, gated0), after=(hidden_low,))
    lefts0_other = swap(lefts0)

    normed1, narrow_pre1, act1, final1, xhat1, rstd1 = front(
        1, pieces, pack1, narrow_w1, after=(lefts0,)
    )
    wide_pre1, lift_low1, *sends = wide1(normed1, d_gated1, pack1, wide_w1, lift_w1, after=(final1,))
    arrived = line(final1)
    parts = scatter(sends)
    enter1, scanned1 = carry(1, act1, arrived, pack1, after=(sends[0],))
    pieces = gather(scanned1)
    d_scanned1, first1 = adjoint_local(1, parts, pack1, after=(scanned1, lefts0_other))
    scanned_all1, gated1, wide_low1 = middle1(pieces, wide_pre1, d_gated1, pack1, lift_w1)
    arrived = line(first1)
    incoming1, narrow_low1 = adjoint(1, d_scanned1, narrow_pre1, arrived, pack1, after=(wide_low1,))
    sends = grad_normed(1, wide_low1, narrow_low1, xhat1, pack1, wide_w1, narrow_w1)
    parts = scatter(sends)
    lefts1 = turn(1, (normed1, scanned_all1, gated1), after=(sends[0],))
    rights1, rights1_give = halve(1, (wide_low1, lift_low1, out_low1), after=(lefts1,))
    lefts1_other, rights1_other = swap(lefts1), swap(rights1_give)
    (late1,) = ssm_grads(
        1,
        act1,
        enter1,
        d_scanned1,
        incoming1,
        lefts1,
        narrow_low1,
        pack1,
        (),
        after=(rights1,),
    )
    grad_mid, grad_low = layer_grad(1, parts, rstd1, xhat1, out_cotangent, pack1, after=(late1,))
    pieces = gather(grad_low)
    weights1 = weight_grads(
        1, (lefts1, lefts1_other), (rights1, rights1_other), after=(grad_low,)
    )
    big1 = to_pairs(weights1, 0)

    top_keep, top_give = top_parts(gated1, down_w1, after=(weights1[0],))
    top_arrived = paired(top_give, "tensor", 1)

    wide_low0, lift_low0, out_low0, *sends = grad_middle0(
        pieces, wide_pre0, lifted0, down_w0, lift_w0, after=(weights1[0], top_keep)
    )
    parts = scatter(sends)
    rights0, rights0_give = halve(0, (wide_low0, lift_low0, out_low0), after=())
    rights0_other = swap(rights0_give)
    for step in range(1, STEPS):
        weights1 = blocks_join(1, weights1, big1, (rights0,))
        big1 = to_pairs(weights1, step)
    d_scanned0, first0 = adjoint_local(0, parts, pack0, after=(rights0, weights1[0]))
    arrived = line(first0)
    weights0 = weight_grads(
        0, (lefts0, lefts0_other), (rights0, rights0_other), after=(first0,)
    )
    big0 = to_pairs(weights0, 0)
    incoming0, narrow_low0 = adjoint(
        0, d_scanned0, narrow_pre0, arrived, pack0, after=(weights0[0], *big1)
    )
    sends = grad_normed(
        0, wide_low0, narrow_low0, xhat0, pack0, wide_w0, narrow_w0
    )
    parts = scatter(sends)
    for step in range(1, STEPS):
        weights0 = blocks_join(0, weights0, big0, (sends[0], top_arrived))
        big0 = to_pairs(weights0, step)
    late, late_give = ssm_grads(
        0,
        act0,
        enter0,
        d_scanned0,
        incoming0,
        lefts0,
        narrow_low0,
        pack0,
        (late1,),
        after=(weights0[0],),
    )
    (sum1,) = big_sum(1, weights1, big1, (), after=(late,))
    top = paired_sum(1, top_keep, top_give, top_arrived, (late,))
    grad, grad_give = layer_grad(
        0, parts, rstd0, xhat0, grad_mid, pack0, after=(late, sum1, top[0], *big0)
    )
    grad_other = swap(grad_give)
    small_parts = late_join(late, swap(late_give), grad, grad_other, after=())
    small_parts_in = scatter(small_parts, "dp")
    keep, give = big_sum(0, weights0, big0, (sum1,), after=(small_parts[0],))
    big_other = swap(give)
    *own, input_grad = own_columns(keep, grad, grad_other, after=())
    output, output_give = layer_output(1, hidden, top, pack1, after=(own[0],))
    (
        by_wide,
        by_lift,
        by_down,
        wide_b,
        lift_b,
        down_b,
        by_narrow,
        narrow_b,
        by_decay,
        by_input,
        by_output,
        by_skip,
        gain,
        shift,
        section_output,
    ) = finish(own, (keep, big_other), late_sum(small_parts_in), output, swap(output_give))
    return (
        section_output,
        input_grad,
        gain,
        shift,
        by_wide,
        wide_b,
        by_narrow,
        narrow_b,
        by_decay,
        by_input,
        by_output,
        by_skip,
        by_lift,
        lift_b,
        by_down,
        down_b,
    )


def solution(mesh):
    placed = (
        P(None, "dp", None),
        P(None, "dp", None),
        P(),
        P("section", None),
        P("section", None),
        P("section", None, "tensor"),
        P("section", "tensor"),
        P("section", None, "tensor"),
        P("section", "tensor"),
        P("section", "tensor", None),
        P("section", "tensor", None),
        P("section", "tensor", None),
        P("section", "tensor"),
        P("section", None, "tensor"),
        P("section", "tensor"),
        P("section", "tensor", None),
        P("section", None),
    )
    return jax.shard_map(
        local,
        mesh=mesh,
        in_specs=placed,
        out_specs=(
            P("section", None, "dp", "tensor"),
            P("section", None, "dp", "tensor"),
            P("section", ("tensor", "dp")),
            P("section", ("tensor", "dp")),
            P("section", "dp", "tensor"),
            P("section", ("tensor", "dp")),
            P("section", "dp", "tensor"),
            P("section", ("tensor", "dp")),
            P("section", ("tensor", "dp"), None),
            P("section", ("tensor", "dp"), None),
            P("section", ("tensor", "dp"), None),
            P("section", ("tensor", "dp")),
            P("section", "dp", "tensor"),
            P("section", ("tensor", "dp")),
            P("section", ("tensor", "dp"), None),
            P("section", "dp"),
        ),
        check_vma=False,
    )
```

```python
from functools import partial

import jax
import jax.numpy as jnp
from jax import lax
from jax.experimental import pallas as pl
from jax.experimental.pallas import tpu as pltpu
from jax.sharding import PartitionSpec as P

F32, BF16 = jnp.float32, jnp.bfloat16
NORM_EPSILON = 1e-05
LANES = 128
GELU_SCALE, GELU_CUBE = 0.7978845608028654, 0.044715
GAIN, SHIFT, DOWN_B, WIDE_B, LIFT_B, NARROW_B, SKIP = 0, 8, 16, 24, 30, 36, 37
MEGA = 1024 * 1024
SPAN = 40_000_000_000
SEGMENTS = 4
IN_VMEM = pl.BlockSpec(memory_space=pltpu.VMEM)
IN_SMEM = pl.BlockSpec(memory_space=pltpu.SMEM)
IN_PLACE = pl.BlockSpec(memory_space=pl.ANY)
IN_HBM = pl.BlockSpec(memory_space=pltpu.HBM)


def mm(left, right):
    return jnp.dot(left, right, preferred_element_type=F32)


def mm_last(left, right):
    return lax.dot_general(left, right, (((1,), (1,)), ((), ())), preferred_element_type=F32)


def mm_first(left, right, precision=None):
    return lax.dot_general(
        left, right, (((0,), (0,)), ((), ())), preferred_element_type=F32, precision=precision
    )


def gelu(z):
    return 0.5 * z * (1.0 + jnp.tanh(GELU_SCALE * (z + GELU_CUBE * z * z * z)))


def gelu_slope(z):
    square = z * z
    bend = jnp.tanh(GELU_SCALE * (z + GELU_CUBE * z * square))
    return 0.5 * (1.0 + bend) + 0.5 * z * (1.0 - bend * bend) * GELU_SCALE * (
        1.0 + 3.0 * GELU_CUBE * square
    )


class Kernel:
    def __init__(self, lengths, length, layer):
        self.lengths, self.length, self.layer = lengths, length, layer

    def __call__(
        self, name, body, outs, vin=(), places=(), picked=(), scratch=(), after=(), spare=6, span=1, keep=False, direct=(), onto=0
    ):
        n_v, n_a, n_p, n_o, n_s = len(vin), len(places), len(picked), len(outs), len(scratch)
        n_w, n_k = len(after), len(picked) if keep else 0
        layer = self.layer

        def run(*refs):
            k = KernelRefs()
            k.meta = placing(refs[0], self.length)
            at = 1
            k.vin = refs[at : at + n_v]
            at += n_v
            k.places = refs[at : at + n_a]
            at += n_a
            pairs = refs[at : at + 2 * n_p]
            at += 2 * n_p + n_w
            k.outs = refs[at : at + n_o]
            at += n_o
            buffers = refs[at : at + n_k]
            at += n_k
            k.scratch = refs[at : at + n_s]
            at += n_s
            if not keep:
                buffers = refs[at : at + n_p]
                at += n_p
            if n_p:
                sems = refs[at]
                mine = k.meta[0] == layer

                def fetch(source):
                    for i in range(n_p):
                        pltpu.make_async_copy(pairs[2 * i + source], buffers[i], sems.at[i]).start()

                pl.when(mine)(partial(fetch, 0))
                pl.when(jnp.logical_not(mine))(partial(fetch, 1))

                def get(i):
                    pltpu.make_async_copy(pairs[2 * i], buffers[i], sems.at[i]).wait()
                    return buffers[i]

                k.get = get
            body(k)

        extra = [] if keep else [pltpu.VMEM(own.shape, own.dtype) for own, _ in picked]
        if n_p:
            extra.append(pltpu.SemaphoreType.DMA((n_p,)))
        held = sum(
            _size(ref.shape) * ref.dtype.itemsize
            for ref in (*scratch, *extra)
            if ref.memory_space == pltpu.VMEM
        )
        flat = [part for pair in picked for part in pair]
        operands = (self.lengths, *vin, *places, *flat, *after)
        return pl.pallas_call(
            run,
            out_shape=[jax.ShapeDtypeStruct(s, d) for s, d in outs]
            + [jax.ShapeDtypeStruct(own.shape, own.dtype) for own, _ in picked[:n_k]],
            in_specs=[IN_SMEM]
            + [IN_VMEM] * n_v
            + [IN_PLACE] * n_a
            + [IN_HBM] * (2 * n_p)
            + [IN_PLACE] * n_w,
            out_specs=[IN_PLACE if i in direct else IN_VMEM for i in range(n_o + n_k)],
            input_output_aliases={1 + n_v + i: i for i in range(onto)},
            scratch_shapes=[*scratch, *extra],
            compiler_params=pltpu.CompilerParams(vmem_limit_bytes=held + spare * MEGA),
            cost_estimate=pl.CostEstimate(flops=span, bytes_accessed=1, transcendentals=0),
            name=name,
        )(*operands)


class KernelRefs:
    pass


def placing(lengths, length):
    section, ti, di = (lax.axis_index(axis) for axis in ("section", "tensor", "dp"))
    first = -di * length
    second = first + lengths[section, 0]
    return [section, ti, di, first, second, second + lengths[section, 1]]


def _size(shape):
    total = 1
    for extent in shape:
        total *= extent
    return total


def vec(pack, first, count):
    column = pack.shape[1] - LANES
    rows = [pack[first + i : first + i + 1, column:] for i in range(count)]
    return rows[0] if count == 1 else jnp.concatenate(rows, axis=1)


def tables(pack):
    return [pack[:, i * LANES : (i + 1) * LANES] for i in range(4)]


def start_in(meta, first, count):
    hit = False
    for i in range(3):
        hit = jnp.logical_or(hit, (meta[3 + i] >= first) & (meta[3 + i] < first + count))
    return hit


def keep_at(meta, place):
    return jnp.where(start_in(meta, place, 1), 0.0, 1.0)


BLOCK = 32


def scan_blocks(meta, length, carry, step, backward=False, block=BLOCK):
    blocks = length // block

    def one(i, carry):
        t0 = pl.multiple_of((blocks - 1 - i if backward else i) * block, block)
        return lax.cond(
            start_in(meta, t0, block),
            lambda c: step(t0, c, True),
            lambda c: step(t0, c, False),
            carry,
        )

    return lax.fori_loop(0, blocks, one, carry)


def row_groups(ref, t0, block, backward=False):
    groups = range(0, block, 8)
    for g in reversed(groups) if backward else groups:
        rows = ref[pl.ds(t0 + g, 8), :]
        for j in reversed(range(8)) if backward else range(8):
            yield g + j, rows[j : j + 1, :]


def end_state(meta, ref, decay, length, backward=False):
    span = length // SEGMENTS
    a = jnp.exp(-decay)

    def step(i, carried, masked):
        out = []
        for g, state in enumerate(carried):
            t0 = pl.multiple_of(g * span + i * 8, 8)
            for j, row in row_groups(ref, t0, 8, backward):
                if backward:
                    state = a * (state + row)
                    if masked:
                        state = state * keep_at(meta, t0 + j)
                else:
                    if masked:
                        state = state * keep_at(meta, t0 + j)
                    state = a * state + row
            out.append(state)
        return tuple(out)

    def one(i, carried):
        i = span // 8 - 1 - i if backward else i
        hit = False
        for g in range(SEGMENTS):
            hit = jnp.logical_or(hit, start_in(meta, g * span + i * 8, 8))
        return lax.cond(hit, lambda c: step(i, c, True), lambda c: step(i, c, False), carried)

    zero = jnp.zeros_like(decay)
    ends = lax.fori_loop(0, span // 8, one, (zero,) * SEGMENTS)
    across = jnp.exp(decay * (-float(span)))
    order = range(SEGMENTS)
    total = zero
    for g in reversed(order) if backward else order:
        through = jnp.where(start_in(meta, g * span, span), 0.0, 1.0)
        total = ends[g] + through * across * total
    return total


def one_minus_exp(d):
    series = 1.0
    for k in range(8, 1, -1):
        series = 1.0 - d * (1.0 / k) * series
    return jnp.where(d < 0.25, d * series, 1.0 - jnp.exp(-d))


def crossing(meta, arrived, decay, length, direction):
    total = jnp.zeros_like(decay)
    for s, part in enumerate(arrived):
        apart = direction * (meta[2] - jnp.bitwise_xor(meta[2], s + 1)) - 1
        first = -apart * length if direction == 1 else length
        open_way = jnp.logical_and(apart >= 0, jnp.logical_not(start_in(meta, first, apart * length)))
        reach = jnp.exp(decay * (-float(length)) * jnp.maximum(apart, 0).astype(F32))
        total = total + jnp.where(open_way, reach * part[...], 0.0)
    return total


def local(
    layer_input,
    out_cotangent,
    seq_lengths,
    norm_gain,
    norm_bias,
    wide_weight,
    wide_bias,
    narrow_weight,
    narrow_bias,
    ssm_decay,
    ssm_input,
    ssm_output,
    ssm_skip,
    lift_weight,
    lift_bias,
    down_weight,
    down_bias,
):
    section = lax.axis_index("section")
    nt, nd = lax.axis_size("tensor"), lax.axis_size("dp")
    T, D = layer_input.shape[1], layer_input.shape[2]
    FW = wide_weight.shape[2]
    HC = narrow_weight.shape[2]
    H = lift_weight.shape[1]
    N = ssm_decay.shape[2]
    DC = D // nt
    kernels = [Kernel(seq_lengths, T, 0), Kernel(seq_lengths, T, 1)]

    flip = [(0, 1), (1, 0)]

    def swap(x):
        return lax.ppermute(x, "section", flip)

    def make_pack():
        vectors = (
            (norm_gain, GAIN),
            (norm_bias, SHIFT),
            (down_bias, DOWN_B),
            (wide_bias, WIDE_B),
            (lift_bias, LIFT_B),
            (narrow_bias, NARROW_B),
            (ssm_skip, SKIP),
        )
        sources = [ssm_decay, ssm_input, ssm_output]
        sources = [jnp.swapaxes(part, 1, 2)[0] for part in sources]

        def body(k):
            pack, held, sems = k.outs[0], k.scratch[:-1], k.scratch[-1]
            copies = [
                pltpu.make_async_copy(source, target, sems.at[i])
                for i, (source, target) in enumerate(zip(k.places, held))
            ]
            for copy in copies:
                copy.start()
            column = 4 * LANES
            pack[:, column:] = jnp.zeros((N, LANES), F32)
            for copy in copies:
                copy.wait()
            for i, source in zip((0, 2, 3), held):
                pack[:, i * LANES : (i + 1) * LANES] = source[...]
            pack[:, LANES : 2 * LANES] = one_minus_exp(held[0][...])
            for (source, first), ref in zip(vectors, held[3:]):
                for i in range(source.shape[1] // LANES):
                    pack[first + i : first + i + 1, column:] = ref[
                        :, i * LANES : (i + 1) * LANES
                    ]

        places = (*sources, *(v for v, _ in vectors))
        return kernels[0](
            "make_pack",
            body,
            [((N, 5 * LANES), F32)],
            places=places,
            scratch=[pltpu.VMEM(part.shape, F32) for part in places]
            + [pltpu.SemaphoreType.DMA((len(places),))],
            spare=56,
            span=SPAN,
        )[0]

    pack = make_pack()
    pack_other = swap(pack)
    narrow_w = (narrow_weight[0], swap(narrow_weight[0]))
    wide_w = (wide_weight[0], swap(wide_weight[0]))
    lift_w = (lift_weight[0], swap(lift_weight[0]))
    down_w = (down_weight[0], swap(down_weight[0]))

    def paired(part, axis, s):
        n = lax.axis_size(axis)
        return lax.ppermute(part, axis, [(i, i ^ s) for i in range(n)])

    def scatter(parts, axis="tensor"):
        n = len(parts)
        return (parts[0], *(paired(parts[s], axis, n - s) for s in range(1, n)))

    def gather(part, forward=False):
        if forward and nt == 4:
            across = paired(part, "tensor", 2)
            beside = paired(part, "tensor", 1)
            return (part, beside, across, paired(across, "tensor", 1))
        return (part, *(paired(part, "tensor", s) for s in range(1, nt)))

    def paired_parts(meta, keep, give, part):
        for i in range(nt // 2):
            for bit, out in ((0, keep), (1, give)):
                out[i] = part(jnp.bitwise_xor(meta[1], 2 * i + bit)).astype(out.dtype)

    def paired_outs(width):
        return [((nt // 2, T, width), F32), ((nt // 2, T, width), BF16)]

    def parts_join(layer, keep, arrived, base, after):
        half, width = keep.shape[0] // 2, keep.shape[2]

        def body(k):
            for i in range(2 * half):
                part = k.vin[0][i] + k.vin[1][i].astype(F32)
                if base and i == 0:
                    part = part + k.vin[2][...] + column_rows(k.vin[3], DOWN_B, k.meta[1])
                out = k.outs[i % 2]
                out[i // 2] = part.astype(out.dtype)

        return kernels[layer](
            f"parts_join{layer}",
            body,
            [((half, T, width), F32), ((half, T, width), BF16)],
            vin=(keep, arrived, *base),
            after=after,
        )

    def paired_sum(layer, keep, give, arrived, base, after):
        step = 2
        while step < nt:
            keep, give = parts_join(layer, keep, arrived, base if step == 2 else (), after)
            arrived = paired(give, "tensor", step)
            step *= 2
        return keep, arrived

    def line(value):
        return tuple(paired(value, "dp", s + 1) for s in range(nd - 1))

    def target(mine, s, n):
        return jnp.bitwise_xor(mine, (n - s) % n)

    HALVES = (FW // 2, FW // 2, D // 2)
    RIGHT = sum(HALVES)

    def turn(layer, sources, after):
        def body(k):
            row = 0
            for source in k.vin:
                for c in range(0, source.shape[1], 256):
                    block = source[:, c : c + 256].astype(F32)
                    k.outs[0][row : row + 256, :] = jnp.transpose(block).astype(BF16)
                    row += 256

        height = sum(part.shape[1] for part in sources)
        return kernels[layer](f"turn{layer}", body, [((height, T), BF16)], vin=sources, after=after)[0]

    def halve(layer, sources, after):
        def body(k):
            at = 0
            for source, width in zip(k.vin, HALVES):
                for out, which in zip(k.outs, (k.meta[0], 1 - k.meta[0])):
                    here = pl.ds(pl.multiple_of(which * width, LANES), width)
                    out[:, at : at + width] = source[:, here]
                at += width

        return kernels[layer](
            f"halve{layer}", body, [((T, RIGHT), BF16)] * 2, vin=sources, after=after
        )

    def choose(layer, pairs, after):
        def body(k):
            for i in range(len(pairs)):
                k.get(i)

        return kernels[layer](f"choose{layer}", body, [], picked=pairs, after=after, keep=True, spare=30)

    def norm_rows(rows, emit):
        def block(i, _):
            here = pl.ds(pl.multiple_of(i * 32, 32), 32)
            x = rows[here, :].astype(F32)
            offset = x - jnp.mean(x, axis=1, keepdims=True)
            spread = jnp.mean(offset * offset, axis=1, keepdims=True)
            inverse = lax.rsqrt(spread + NORM_EPSILON)
            emit(here, offset * inverse, inverse)
            return 0

        lax.fori_loop(0, T // 32, block, 0, unroll=4)

    def norm0(after):
        def body(k):
            xhat, rstd = k.outs
            rows, sems = k.scratch
            copy = pltpu.make_async_copy(k.places[0].at[k.meta[0]], rows, sems.at[0])
            copy.start()
            copy.wait()

            def emit(here, standard, inverse):
                xhat[here, :] = standard
                rstd[here, :] = jnp.broadcast_to(inverse, (32, LANES))

            norm_rows(rows, emit)

        return kernels[0](
            "norm0",
            body,
            [((T, D), F32), ((T, LANES), F32)],
            places=(layer_input,),
            after=after,
            scratch=[pltpu.VMEM((T, D), BF16), pltpu.SemaphoreType.DMA((1,))],
            span=SPAN,
        )

    def front(layer, source, pack, narrow, after=()):
        def body(k):
            meta = k.meta
            normed, narrow_pre, act, final = k.outs[:4]
            if layer == 0:
                pk, upper = k.outs[4:]
                keep_or_give(meta, pk, upper, k.vin[1][...], k.vin[2][...], False)
            else:
                xhat, rstd = k.outs[4:]
                rows = k.scratch[0]
                assemble(meta, k.vin, rows)
                pk, weight = k.vin[nt:]
            gain, shift = vec(pk, GAIN, D // LANES), vec(pk, SHIFT, D // LANES)
            if layer == 0:
                for r in range(0, T, 32):
                    here = slice(r, r + 32)
                    normed[here, :] = (k.vin[0][here, :] * gain + shift).astype(BF16)
                weight = k.get(0)
            else:

                def emit(here, standard, inverse):
                    xhat[here, :] = standard
                    rstd[here, :] = jnp.broadcast_to(inverse, (32, LANES))
                    normed[here, :] = (standard * gain + shift).astype(BF16)

                norm_rows(rows, emit)
            pre = mm(normed[...], weight[...]) + vec(pk, NARROW_B, 1)
            narrow_pre[...] = pre
            act[...] = gelu(pre)
            final[...] = end_state(meta, act, tables(pk)[0], T)

        return kernels[layer](
            f"front{layer}",
            body,
            [((T, D), BF16), ((T, HC), F32), ((T, HC), F32), ((N, HC), F32)]
            + (
                [(pack[0].shape, F32)] * 2
                if layer == 0
                else [((T, D), F32), ((T, LANES), F32)]
            ),
            after=after,
            vin=(source, *pack) if layer == 0 else (*source, pack, narrow),
            picked=(narrow,) if layer == 0 else (),
            keep=True,
            scratch=[] if layer == 0 else [pltpu.VMEM((T, D), BF16)],
            span=SPAN,
        )

    def wide0(normed, pack):
        def body(k):
            bias = vec(k.vin[1], WIDE_B, FW // LANES)
            weight = k.get(0)
            for c in range(0, FW, 256):
                k.outs[0][:, c : c + 256] = (
                    mm(k.vin[0][...], weight[:, c : c + 256]) + bias[:, c : c + 256]
                )

        return kernels[0](
            "wide0",
            body,
            [((T, FW), F32)],
            vin=(normed, pack),
            picked=(wide_w,),
            keep=True,
            spare=6,
        )

    def wide1(normed, d_gated, pack, wide, lift, after):
        def body(k):
            wide_pre, lift_low = k.outs[:2]
            pk, weight, lift = k.vin[2:]
            bias = vec(pk, WIDE_B, FW // LANES)
            for c in range(0, FW, 256):
                pre = mm(k.vin[0][...], weight[:, c : c + 256]) + bias[:, c : c + 256]
                wide_pre[:, c : c + 256] = pre
                lift_low[:, c : c + 256] = (k.vin[1][:, c : c + 256] * gelu(pre)).astype(BF16)
            lift_parts(k.meta, lift_low, lift, k.outs[2:])

        return kernels[1](
            "wide1",
            body,
            [((T, FW), F32), ((T, FW), BF16)] + parted(HC),
            vin=(normed, d_gated, pack, wide, lift),
            after=after,
            span=SPAN,
        )

    def parted(width, rows=T):
        return [((rows, width), F32)] + [((rows, width), BF16)] * (nt - 1)

    def lift_parts(meta, lift_low, lift, sends):
        for s in range(nt):
            at = target(meta[1], s, nt) * HC
            part = mm_last(lift_low[...], lift[pl.ds(pl.multiple_of(at, HC), HC), :])
            sends[s][...] = part.astype(sends[s].dtype)

    def carry(layer, act, arrived, pack, after=()):
        def body(k):
            meta = k.meta
            u = k.vin[0]
            entering, scanned = k.outs
            local_out = k.scratch[0]
            pk = k.vin[1]
            decay, grown, rate_in, read_out = tables(pk)
            skip = vec(pk, SKIP, 1)
            a, read = jnp.exp(-decay), read_out * rate_in * grown
            state = crossing(meta, k.vin[2:], decay, T, 1)
            entering[...] = state

            def step(t0, state, masked):
                outs = []
                for j, row in row_groups(u, t0, BLOCK):
                    if masked:
                        state = state * keep_at(meta, t0 + j)
                    state = a * state + row
                    outs.append(jnp.sum(read * state, axis=0, keepdims=True) + skip * row)
                for g in range(0, BLOCK, 8):
                    local_out[pl.ds(t0 + g, 8), :] = jnp.concatenate(outs[g : g + 8], axis=0)
                return state

            scan_blocks(meta, T, state, step)
            scanned[...] = local_out[...].astype(BF16)

        return kernels[layer](
            f"carry{layer}",
            body,
            [((N, HC), F32), ((T, HC), BF16)],
            vin=(act, pack, *arrived),
            after=after,
            scratch=[pltpu.VMEM((T, HC), F32)],
            span=SPAN,
        )

    def assemble(meta, parts, whole):
        width = parts[0].shape[1]
        for s in range(nt):
            at = jnp.bitwise_xor(meta[1], s) * width
            whole[:, pl.ds(pl.multiple_of(at, width), width)] = parts[s][...]

    def down_parts(meta, gated, down, sends):
        for s in range(nt):
            at = target(meta[1], s, nt) * DC
            part = mm(gated[...], down[:, pl.ds(pl.multiple_of(at, DC), DC)])
            sends[s][...] = part.astype(sends[s].dtype)

    def middle0(pieces, wide_pre, pack, lift, down):
        def body(k):
            scanned, lifted, gated = k.outs[:3]
            assemble(k.meta, k.vin[:nt], scanned)
            wide_pre, pk, lift, down = k.vin[nt:]
            bias = vec(pk, LIFT_B, FW // LANES)
            for c in range(0, FW, 256):
                part = mm(scanned[...], lift[:, c : c + 256]) + bias[:, c : c + 256]
                lifted[:, c : c + 256] = part
                gated[:, c : c + 256] = (part * gelu(wide_pre[:, c : c + 256])).astype(BF16)
            down_parts(k.meta, gated, down, k.outs[3:])

        return kernels[0](
            "middle0",
            body,
            [((T, H), BF16), ((T, FW), F32), ((T, FW), BF16)] + parted(DC),
            vin=(*pieces, wide_pre, pack, lift, down),
            span=SPAN,
        )

    def middle1(pieces, wide_pre, d_gated, pack, lift):
        def body(k):
            scanned, gated, wide_low = k.outs
            assemble(k.meta, k.vin[:nt], scanned)
            pre, grad, pk, lift = k.vin[nt:]
            bias = vec(pk, LIFT_B, FW // LANES)
            for c in range(0, FW, 256):
                part = mm(scanned[...], lift[:, c : c + 256]) + bias[:, c : c + 256]
                z = pre[:, c : c + 256]
                gated[:, c : c + 256] = (part * gelu(z)).astype(BF16)
                wide_low[:, c : c + 256] = (grad[:, c : c + 256] * part * gelu_slope(z)).astype(BF16)

        return kernels[1](
            "middle1",
            body,
            [((T, H), BF16), ((T, FW), BF16), ((T, FW), BF16)],
            vin=(*pieces, wide_pre, d_gated, pack, lift),
            span=SPAN,
        )

    def top_parts(gated, down, after):
        def body(k):
            gated, down = k.vin
            paired_parts(
                k.meta,
                *k.outs,
                lambda at: mm(gated[...], down[:, pl.ds(pl.multiple_of(at * DC, DC), DC)]),
            )

        return kernels[1]("top_parts", body, paired_outs(DC), vin=(gated, down), after=after)

    def column_rows(pk, first, at):
        per = DC // LANES
        best = vec(pk, first, per)
        for i in range(1, nt):
            best = jnp.where(at == i, vec(pk, first + i * per, per), best)
        return best

    def keep_or_give(meta, keep, give, first, second, by_layer=True):
        lower = meta[0] == 0
        keep[...] = jnp.where(lower, first, second)
        give[0 : keep.shape[0], :] = jnp.where(lower, second, first).astype(give.dtype)

    def layer_output(layer, before, parts, pack, after=()):
        def body(k):
            meta = k.meta
            if layer == 0:
                rows = k.scratch[0]
                copy = pltpu.make_async_copy(
                    k.places[0].at[meta[0], :, pl.ds(pl.multiple_of(meta[1] * DC, DC), DC)],
                    rows,
                    k.scratch[1].at[0],
                )
                copy.start()
                copy.wait()
                total = rows[...].astype(F32)
                for part in k.vin[1:]:
                    total = total + part[...].astype(F32)
                total = total + column_rows(k.vin[0], DOWN_B, meta[1])
            else:
                total = k.vin[1][0] + k.vin[2][0].astype(F32)
            if layer == 0:
                k.outs[0][...] = total
                k.outs[1][...] = total.astype(BF16)
            else:
                k.outs[0][...] = total

        return kernels[layer](
            f"layer_output{layer}",
            body,
            [((T, DC), F32)] + ([((T, DC), BF16)] if layer == 0 else []),
            vin=(pack, *parts),
            after=after,
            places=(before,) if layer == 0 else (),
            scratch=[pltpu.VMEM((T, DC), BF16), pltpu.SemaphoreType.DMA((1,))] if layer == 0 else [],
            span=1 if layer else SPAN,
        )

    def grad_gated1(down, after):
        def body(k):
            rows = k.outs[1]
            copy = pltpu.make_async_copy(k.places[0].at[k.meta[0]], rows, k.scratch[0].at[0])
            copy.start()
            copy.wait()
            down = k.vin[0]
            for c in range(0, FW, 256):
                k.outs[0][:, c : c + 256] = mm_last(rows[...], down[c : c + 256, :])

        return kernels[1](
            "grad_gated1",
            body,
            [((T, FW), F32), ((T, D), BF16)],
            places=(out_cotangent,),
            vin=(down,),
            after=after,
            scratch=[pltpu.SemaphoreType.DMA((1,))],
        )

    def grad_middle0(pieces, wide_pre, lifted, down, lift, after=()):
        def body(k):
            wide_low, low, rows = k.outs[:3]
            pre, raised, down, lift = k.vin[nt:]
            assemble(k.meta, k.vin[:nt], rows)
            for c in range(0, FW, 256):
                grad = mm_last(rows[...], down[c : c + 256, :])
                z = pre[:, c : c + 256]
                low[:, c : c + 256] = (grad * gelu(z)).astype(BF16)
                wide_low[:, c : c + 256] = (
                    grad * raised[:, c : c + 256] * gelu_slope(z)
                ).astype(BF16)
            lift_parts(k.meta, low, lift, k.outs[3:])

        return kernels[0](
            "grad_middle0",
            body,
            [((T, FW), BF16), ((T, FW), BF16), ((T, D), BF16)] + parted(HC),
            vin=(*pieces, wide_pre, lifted, down, lift),
            after=after,
            span=SPAN,
        )

    def adjoint_local(layer, parts, pack, after=()):
        def body(k):
            grads, first = k.outs
            total = k.vin[1][...]
            for part in k.vin[2:]:
                total = total + part[...].astype(F32)
            grads[...] = total
            first[...] = end_state(k.meta, grads, tables(k.vin[0])[0], T, backward=True)

        return kernels[layer](
            f"adjoint_local{layer}",
            body,
            [((T, HC), F32), ((N, HC), F32)],
            vin=(pack, *parts),
            after=after,
            span=SPAN,
        )

    def adjoint(layer, d_scanned, narrow_pre, arrived, pack, after=()):
        def body(k):
            meta = k.meta
            grads, pre, pk = k.vin[:3]
            after, narrow_low = k.outs
            d_narrow = k.scratch[0]
            decay, grown, rate_in, read_out = tables(pk)
            skip = vec(pk, SKIP, 1)
            a, read = jnp.exp(-decay), read_out * rate_in * grown
            incoming = crossing(meta, k.vin[3:], decay, T, -1)
            after[...] = incoming

            def step(t0, z, masked):
                outs = [None] * BLOCK
                for j, row in row_groups(grads, t0, BLOCK, True):
                    w = z + row
                    outs[j] = jnp.sum(read * w, axis=0, keepdims=True) + skip * row
                    z = a * w
                    if masked:
                        z = z * keep_at(meta, t0 + j)
                for g in range(0, BLOCK, 8):
                    d_narrow[pl.ds(t0 + g, 8), :] = jnp.concatenate(outs[g : g + 8], axis=0)
                return z

            scan_blocks(meta, T, incoming, step, backward=True)
            narrow_low[...] = (d_narrow[...] * gelu_slope(pre[...])).astype(BF16)

        return kernels[layer](
            f"adjoint{layer}",
            body,
            [((N, HC), F32), ((T, HC), BF16)],
            vin=(d_scanned, narrow_pre, pack, *arrived),
            after=after,
            scratch=[pltpu.VMEM((T, HC), F32)],
            span=SPAN,
        )

    LATE = D // 2 + 2 * N

    def states_before(layer, act, entering, pack, after):
        def body(k):
            u, enter, pk = k.vin
            a = jnp.exp(-tables(pk)[0])

            def ahead(t0, state, masked):
                for j, row in row_groups(u, t0, BLOCK):
                    if masked:
                        state = state * keep_at(k.meta, t0 + j)
                    k.outs[0][t0 + j] = state
                    state = a * state + row
                return state

            scan_blocks(k.meta, T, enter[...], ahead)

        return kernels[layer](
            f"states_before{layer}",
            body,
            [((T, N, HC), F32)],
            vin=(act, entering, pack),
            after=after,
        )[0]

    def ssm_grads(layer, act, states, d_scanned, incoming, turned, narrow_low, pack, upper, after):
        def body(k):
            meta = k.meta
            u, states, grads, incoming, low, pk = k.vin[:6]
            lefts, sems = k.scratch[:2]
            late = k.outs[0] if layer == 1 else k.scratch[2]
            copy = pltpu.make_async_copy(k.places[0].at[0:D, :], lefts, sems.at[0])
            copy.start()
            decay, grown, rate_in, read_out = tables(pk)
            a = jnp.exp(-decay)
            zero = jnp.zeros((N, HC), F32)

            def back(t0, carried, masked):
                z, with_rows, with_states = carried
                rows = row_groups(u, t0, BLOCK, True)
                for (j, row), (_, grad) in zip(rows, row_groups(grads, t0, BLOCK, True)):
                    w = z + grad
                    with_rows = with_rows + w * row
                    with_states = with_states + w * states[t0 + j]
                    z = a * w
                    if masked:
                        z = z * keep_at(meta, t0 + j)
                return z, with_rows, with_states

            _, with_rows, with_states = scan_blocks(
                meta, T, (incoming[...], zero, zero), back, backward=True
            )
            b = rate_in * grown
            first, second = slice(D // 2, D // 2 + N), slice(D // 2 + N, D // 2 + 2 * N)
            late[first, 0:LANES] = a * read_out * (rate_in * with_rows - b * with_states)
            late[first, LANES:] = grown * read_out * with_rows
            late[second, 0:LANES] = b * with_rows
            late[second, LANES:] = zero
            row = D // 2 + N
            late[row : row + 1, LANES:] = jnp.sum(low[...].astype(F32), axis=0, keepdims=True)
            late[row + 1 : row + 2, LANES:] = jnp.sum(u[...] * grads[...], axis=0, keepdims=True)
            copy.wait()
            for h in range(2):
                late[0 : D // 2, h * LANES : (h + 1) * LANES] = mm(
                    lefts[h * (D // 2) : (h + 1) * (D // 2), :], low[...]
                )
            if layer == 0:
                keep_or_give(meta, k.outs[0], k.outs[1], late[...], k.vin[6][...])

        return kernels[layer](
            f"ssm_grads{layer}",
            body,
            [((LATE, 2 * LANES), F32)] * (2 - layer),
            vin=(act, states, d_scanned, incoming, narrow_low, pack, *upper),
            places=(turned,),
            span=1 if layer else SPAN,
            after=after,
            scratch=[
                pltpu.VMEM((D, T), BF16),
                pltpu.SemaphoreType.DMA((1,)),
            ]
            + ([pltpu.VMEM((LATE, 2 * LANES), F32)] if layer == 0 else []),
        )

    def grad_normed(layer, wide_low, narrow_low, xhat, pack, wide, narrow, after=()):
        def body(k):
            meta = k.meta
            wide_low, narrow_in, standard, gains, wide, narrow = k.vin
            ones = jnp.ones((8, DC), BF16)
            sums = jnp.zeros((16, T), F32)
            for s in range(nt):
                at = target(meta[1], s, nt)
                here = pl.ds(pl.multiple_of(at * DC, DC), DC)
                part = mm_last(wide_low[...], wide[here, :]) + mm_last(
                    narrow_in[...], narrow[here, :]
                )
                scaled = part * column_rows(gains, GAIN, at)
                with_x = scaled * standard[:, here]
                sums = sums + jnp.concatenate(
                    [mm_last(ones, scaled.astype(BF16)), mm_last(ones, with_x.astype(BF16))], axis=0
                )
                k.outs[s][0:T, :] = part.astype(k.outs[s].dtype)
            for s in range(nt):
                k.outs[s][T:, :] = sums.astype(k.outs[s].dtype)

        return kernels[layer](
            f"grad_normed{layer}",
            body,
            parted(DC, T + 16),
            vin=(wide_low, narrow_low, xhat, pack, wide, narrow),
            after=after,
            span=SPAN,
        )

    def layer_grad(layer, parts, rstd, xhat, grad_out, pack, after):
        def body(k):
            meta = k.meta
            here = pl.ds(pl.multiple_of(meta[1] * DC, DC), DC)
            standard, sems = k.scratch[0], k.scratch[1]
            copy = pltpu.make_async_copy(k.places[0].at[:, here], standard, sems.at[0])
            copy.start()
            if layer == 1:
                copy_out = pltpu.make_async_copy(
                    k.places[1].at[meta[0], :, here], k.scratch[2], sems.at[1]
                )
                copy_out.start()
            total, sums = k.vin[0][0:T, :], k.vin[0][T:, :]
            for part in k.vin[1:nt]:
                total = total + part[0:T, :].astype(F32)
                sums = sums + part[T:, :].astype(F32)
            inverse = k.vin[nt]
            row = lax.broadcasted_iota(jnp.int32, (16, LANES), 0)
            first = mm_first(sums, (row == 0).astype(F32), lax.Precision.HIGHEST) * (1.0 / D)
            second = mm_first(sums, (row == 8).astype(F32), lax.Precision.HIGHEST) * (1.0 / D)
            scaled = total * column_rows(k.vin[nt + 1], GAIN, meta[1])
            copy.wait()
            if layer == 1:
                copy_out.wait()
                grad_in = k.scratch[2][...].astype(F32)
            else:
                grad_in = k.vin[nt + 2][...]
            if layer == 1:
                result = k.outs[0]
            else:
                keep, give, upper = k.outs[0], k.outs[1], k.vin[nt + 2]
                result = k.scratch[2]
            for c in range(0, DC, LANES):
                x = standard[:, c : c + LANES]
                grad = grad_in[0:T, c : c + LANES] + inverse[...] * (
                    scaled[:, c : c + LANES] - first - x * second
                )
                result[0:T, c : c + LANES] = grad
                if layer == 1:
                    k.outs[1][:, c : c + LANES] = grad.astype(BF16)
            result[T:, :] = jnp.zeros((8, DC), F32)
            result[T : T + 1, :] = jnp.sum(total * standard[...], axis=0, keepdims=True)
            result[T + 1 : T + 2, :] = jnp.sum(total, axis=0, keepdims=True)
            if layer == 0:
                keep_or_give(meta, keep, give, result[...], upper[...])
                give[T + 8 :, :] = jnp.zeros((8, DC), BF16)

        return kernels[layer](
            f"layer_grad{layer}",
            body,
            [((T + 8, DC), F32), ((T, DC), BF16)]
            if layer == 1
            else [((T + 8, DC), F32), ((T + 16, DC), BF16)],
            after=after,
            vin=(*parts, rstd, pack) + (() if layer == 1 else (grad_out,)),
            places=(xhat,) + ((grad_out,) if layer == 1 else ()),
            scratch=[pltpu.VMEM((T, DC), F32), pltpu.SemaphoreType.DMA((2,))]
            + [pltpu.VMEM((T, DC), BF16) if layer == 1 else pltpu.VMEM((T + 8, DC), F32)],
            span=SPAN,
        )

    RW, RL, RD = D // nd, H // nd, FW // nd
    CW, CD = HALVES[0] // LANES, HALVES[2] // LANES
    AT_L = RW * CW
    AT_D = AT_L + RL * CW
    AT_V = AT_D + RD * CD
    BIG = AT_V + 16
    CUT = AT_L + 2 * RL
    STEPS = nd.bit_length() - 1

    def mirrored(s):
        return sum(((s >> b) & 1) << (STEPS - 1 - b) for b in range(STEPS))

    def block_outs(count):
        return [((count, rows, LANES), BF16) for rows in (CUT, BIG - CUT) for _ in range(2)]

    def to_pairs(blocks, step):
        return (
            paired(blocks[1], "dp", 1 << step),
            paired(blocks[3], "dp", 1 << (STEPS - 1 - step)),
        )

    def blocks_join(layer, blocks, arrived, after):
        count = blocks[0].shape[0] // 2

        def body(k):
            for h in range(2):
                for i in range(2 * count):
                    part = k.vin[2 * h][i].astype(F32) + k.vin[2 * h + 1][i].astype(F32)
                    k.outs[2 * h + i % 2][i // 2] = part.astype(BF16)

        return kernels[layer](
            f"blocks_join{layer}",
            body,
            block_outs(count),
            vin=(blocks[0], arrived[0], blocks[2], arrived[1]),
            after=after,
        )

    def put(k, s, row, value):
        first = row < CUT
        i = s if first else mirrored(s)
        out = k.outs[i % 2 if first else 2 + i % 2]
        row -= 0 if first else CUT
        out[i // 2, row : row + value.shape[0], :] = value.astype(BF16)

    def weight_grads(layer, lefts, rights, after):
        def body(k):
            meta = k.meta
            left, right = k.vin[:2], k.vin[2:]

            def product(row, rows, at, width, at_row):
                columns = slice(at, at + width)
                for s in range(nd):
                    first = row + jnp.bitwise_xor(meta[2], s) * rows
                    here = pl.ds(pl.multiple_of(first, 16), rows)
                    part = mm(left[0][here, :], right[0][:, columns])
                    part = part + mm(left[1][here, :], right[1][:, columns])
                    for h in range(0, width, LANES):
                        put(k, s, at_row + h // LANES * rows, part[:, h : h + LANES])

            product(0, RW, 0, HALVES[0], 0)
            product(D, RL, HALVES[0], HALVES[1], AT_L)
            product(D + H, RD, HALVES[0] + HALVES[1], HALVES[2], AT_D)
            sums = k.scratch[0]
            sums[...] = jnp.zeros((16, LANES), F32)
            for i in range(RIGHT // LANES):
                here = slice(i * LANES, (i + 1) * LANES)
                total = jnp.sum(right[0][:, here].astype(F32), axis=0, keepdims=True)
                total = total + jnp.sum(right[1][:, here].astype(F32), axis=0, keepdims=True)
                sums[i : i + 1, :] = total
            for s in range(nd):
                put(k, s, AT_V, sums[...])

        return kernels[layer](
            f"weight_grads{layer}",
            body,
            block_outs(nd // 2),
            vin=(*lefts, *rights),
            after=after,
            scratch=[pltpu.VMEM((16, LANES), F32)],
        )

    SMALL = RW + 3 * N + 16

    def late_join(keep, other, grad, grad_other, after):
        def body(k):
            meta = k.meta
            own, other, grad, grad_other = k.vin
            rest = k.scratch[0]

            def summed(rows, columns):
                return own[rows, columns] + other[rows, columns]

            half = D // 2
            left, right = slice(0, LANES), slice(LANES, 2 * LANES)
            upper = slice(half, half + N)
            rest[0:N, :] = summed(upper, left)
            rest[N : 2 * N, :] = summed(upper, right)
            rest[2 * N : 3 * N, :] = summed(slice(half + N, half + 2 * N), left)
            rest[3 * N : 3 * N + 8, :] = summed(slice(half + N, half + N + 8), right)
            rest[3 * N + 8 :, :] = jnp.zeros((8, LANES), F32)
            per = DC // LANES
            for i in range(2):
                row = grad[T + i : T + i + 1, :] + grad_other[T : T + 16, :].astype(F32)[i : i + 1, :]
                for h in range(per):
                    first = 3 * N + 8 + i * per + h
                    rest[first : first + 1, :] = row[:, h * LANES : (h + 1) * LANES]
            for s in range(nd):
                at = target(meta[2], s, nd) * RW
                here = pl.ds(pl.multiple_of(lax.rem(at, half), 16), RW)
                for h in range(2):

                    def put(h=h, out=k.outs[s]):
                        columns = slice(h * LANES, (h + 1) * LANES)
                        out[0:RW, :] = summed(here, columns).astype(BF16)

                    pl.when(at // half == h)(put)
                k.outs[s][RW:, :] = rest[...].astype(BF16)

        return kernels[0](
            "late_join",
            body,
            [((SMALL, LANES), BF16)] * nd,
            vin=(keep, other, grad, grad_other),
            after=after,
            scratch=[pltpu.VMEM((3 * N + 16, LANES), F32)],
        )

    def pick(meta, flat, out):
        width = out.shape[1]
        best = flat[:, 0:width]
        for i in range(1, nd):
            best = jnp.where(meta[2] == i, flat[:, i * width : (i + 1) * width], best)
        out[...] = best

    def chunk(meta, source, first, count, out):
        flat = [source[first + i : first + i + 1, :] for i in range(count)]
        pick(meta, flat[0] if count == 1 else jnp.concatenate(flat, axis=1), out)

    def big_sum(layer, blocks, arrived, upper, after):
        def body(k):
            for h, (first, rows) in enumerate(((0, CUT), (CUT, BIG - CUT))):
                for r in range(0, rows, 256):
                    inner = slice(r, min(r + 256, rows))
                    here = slice(first + inner.start, first + inner.stop)
                    total = k.vin[2 * h][0, inner, :].astype(F32)
                    total = total + k.vin[2 * h + 1][0, inner, :].astype(F32)
                    if layer == 1:
                        k.outs[0][here, :] = total
                    else:
                        lower = k.meta[0] == 0
                        other = k.vin[4][here, :]
                        k.outs[0][here, :] = jnp.where(lower, total, other)
                        k.outs[1][here, :] = jnp.where(lower, other, total).astype(BF16)

        return kernels[layer](
            f"big_sum{layer}",
            body,
            [((BIG, LANES), F32)] + ([((BIG, LANES), BF16)] if layer == 0 else []),
            vin=(blocks[0], arrived[0], blocks[2], arrived[1], *upper),
            after=after,
        )

    def late_sum(parts):
        def body(k):
            total = k.vin[0][...].astype(F32)
            for part in k.vin[1:]:
                total = total + part[...].astype(F32)
            k.outs[0][...] = total

        return kernels[0]("late_sum", body, [((SMALL, LANES), F32)], vin=parts, span=SPAN)[0]

    def big_places():
        return ((0, RW, CW), (AT_L, RL, CW), (AT_D, RD, CD))

    def own_columns(keep, grad, grad_other, after):
        def body(k):
            meta = k.meta
            *outs, grads, token = k.outs
            token[...] = jnp.zeros((8, LANES), F32)
            rows, sems = k.scratch
            rows[...] = k.vin[0][0:T, :].astype(F32)
            moves = [(k.places[1].at[0:T, :], grads.at[0, meta[0]]), (rows, grads.at[0, 1 - meta[0]])]
            for out, (first, height, columns) in zip(outs, big_places()):
                for c in range(columns):
                    at = pl.multiple_of((meta[0] * columns + c) * LANES, LANES)
                    moves.append(
                        (
                            k.places[0].at[first + c * height : first + (c + 1) * height, :],
                            out.at[0, :, pl.ds(at, LANES)],
                        )
                    )
            moves = [
                pltpu.make_async_copy(source, out, sems.at[i])
                for i, (source, out) in enumerate(moves)
            ]
            for move in moves:
                move.start()
            for move in moves:
                move.wait()

        return kernels[0](
            "own_columns",
            body,
            [
                ((1, RW, FW), F32),
                ((1, RL, FW), F32),
                ((1, RD, D), F32),
                ((1, 2, T, DC), F32),
                ((8, LANES), F32),
            ],
            vin=(grad_other,),
            places=(keep, grad),
            after=after,
            direct=(0, 1, 2, 3),
            scratch=[pltpu.VMEM((T, DC), F32), pltpu.SemaphoreType.DMA((2 + 2 * CW + CD,))],
        )

    def finish(own, big, small, lower, upper):
        def body(k):
            meta = k.meta
            wide, lift, down, rows, turned, sems = k.scratch
            by_wide, by_lift, by_down = k.outs[:3]
            wide_b, lift_b, down_b = k.outs[3:6]
            by_narrow, narrow_b, *by_ssm, by_skip, gain, shift, outputs = k.outs[6:]
            keep, give, late = k.vin

            def output(layer, i):
                return pltpu.make_async_copy(
                    k.places[3 + 2 * layer + i],
                    outputs.at[0, meta[0] if i == 0 else 1 - meta[0]],
                    sems.at[3 + i],
                )

            def send(layer):
                for i in range(2):
                    output(layer, i).start()

            pl.when(meta[0] == 0)(partial(send, 0))
            pl.when(meta[0] != 0)(partial(send, 1))
            moves = [
                pltpu.make_async_copy(k.places[7].at[0:RW, :], by_narrow.at[0], sems.at[5])
            ]
            moves[0].start()
            moves += [output(0, i) for i in range(2)]
            for q, (buffer, out, (first, height, columns)) in enumerate(
                zip((wide, lift, down), (by_wide, by_lift, by_down), big_places())
            ):
                for c in range(columns):
                    part = give[first + c * height : first + (c + 1) * height, :]
                    buffer[:, c * LANES : (c + 1) * LANES] = part.astype(F32)
                width = columns * LANES
                at = pl.multiple_of((1 - meta[0]) * width, LANES)
                moves.append(
                    pltpu.make_async_copy(buffer, out.at[0, :, pl.ds(at, width)], sems.at[q])
                )
                moves[-1].start()
            lower = meta[0] == 0
            own, other = keep[AT_V:, :], give[AT_V:, :].astype(F32)
            rows[0:16, :] = jnp.where(lower, own, other)
            rows[16:, :] = jnp.where(lower, other, own)
            at = 0
            for columns, out in ((CW, wide_b), (CW, lift_b), (CD, down_b)):
                whole = [rows[h + at + i : h + at + i + 1, :] for h in (0, 16) for i in range(columns)]
                pick(meta, jnp.concatenate(whole, axis=1), out)
                at += columns
            rows[0:16, :] = late[RW + 3 * N :, :]
            chunk(meta, rows, 0, 1, narrow_b)
            chunk(meta, rows, 1, 1, by_skip)
            chunk(meta, rows, 8, DC // LANES, gain)
            chunk(meta, rows, 8 + DC // LANES, DC // LANES, shift)
            per = HC // nd
            for i in range(3):
                turned[...] = jnp.transpose(late[RW + i * N : RW + (i + 1) * N, :])
                by_ssm[i][0] = turned[pl.ds(pl.multiple_of(meta[2] * per, per), per), :]
            for move in moves:
                move.wait()

        return kernels[0](
            "finish",
            body,
            [
                *((part.shape, F32) for part in own),
                ((1, FW // nd), F32),
                ((1, FW // nd), F32),
                ((1, D // nd), F32),
                ((1, RW, HC), F32),
                ((1, HC // nd), F32),
                ((1, HC // nd, N), F32),
                ((1, HC // nd, N), F32),
                ((1, HC // nd, N), F32),
                ((1, HC // nd), F32),
                ((1, DC // nd), F32),
                ((1, DC // nd), F32),
                ((1, 2, T, DC), F32),
            ],
            vin=(*big, small),
            places=(*own, *lower, *upper, small),
            direct=(0, 1, 2, 6, 14),
            onto=3,
            scratch=[
                pltpu.VMEM((RW, HALVES[0]), F32),
                pltpu.VMEM((RL, HALVES[1]), F32),
                pltpu.VMEM((RD, HALVES[2]), F32),
                pltpu.VMEM((32, LANES), F32),
                pltpu.VMEM((HC, N), F32),
                pltpu.SemaphoreType.DMA((6,)),
            ],
        )

    xhat0, rstd0 = norm0(after=())
    normed0, narrow_pre0, act0, final0, pack0, pack1, narrow_w0 = front(
        0, xhat0, (pack, pack_other), narrow_w
    )
    arrived = line(final0)
    wide_pre0, wide_w0 = wide0(normed0, pack0)
    enter0, scanned0 = carry(0, act0, arrived, pack0, after=(wide_pre0,))
    pieces = gather(scanned0)
    lift_w0, down_w0 = choose(0, (lift_w, down_w), after=(scanned0,))
    scanned_all0, lifted0, gated0, *sends = middle0(pieces, wide_pre0, pack0, lift_w0, down_w0)
    parts = scatter(sends)
    narrow_w1, wide_w1, lift_w1, down_w1 = choose(
        1, (narrow_w, wide_w, lift_w, down_w), after=(sends[0],)
    )
    d_gated1, out_low1 = grad_gated1(down_w1, after=(sends[0],))
    hidden, hidden_low = layer_output(0, layer_input, parts, pack0, after=(d_gated1,))
    pieces = gather(hidden_low, forward=True)
    lefts0 = turn(0, (normed0, scanned_all0, gated0), after=(hidden_low,))
    lefts0_other, hidden_other = swap(lefts0), swap(hidden)

    normed1, narrow_pre1, act1, final1, xhat1, rstd1 = front(
        1, pieces, pack1, narrow_w1, after=(lefts0,)
    )
    wide_pre1, lift_low1, *sends = wide1(normed1, d_gated1, pack1, wide_w1, lift_w1, after=(final1,))
    arrived = line(final1)
    parts = scatter(sends)
    enter1, scanned1 = carry(1, act1, arrived, pack1, after=(sends[0],))
    pieces = gather(scanned1)
    d_scanned1, first1 = adjoint_local(1, parts, pack1, after=(scanned1, lefts0_other, hidden_other))
    scanned_all1, gated1, wide_low1 = middle1(pieces, wide_pre1, d_gated1, pack1, lift_w1)
    arrived = line(first1)
    states1 = states_before(1, act1, enter1, pack1, after=(wide_low1,))
    incoming1, narrow_low1 = adjoint(1, d_scanned1, narrow_pre1, arrived, pack1, after=(states1,))
    sends = grad_normed(1, wide_low1, narrow_low1, xhat1, pack1, wide_w1, narrow_w1)
    parts = scatter(sends)
    lefts1 = turn(1, (normed1, scanned_all1, gated1), after=(sends[0],))
    rights1, rights1_give = halve(1, (wide_low1, lift_low1, out_low1), after=(lefts1,))
    lefts1_other, rights1_other = swap(lefts1), swap(rights1_give)
    (late1,) = ssm_grads(
        1,
        act1,
        states1,
        d_scanned1,
        incoming1,
        lefts1,
        narrow_low1,
        pack1,
        (),
        after=(rights1,),
    )
    grad_mid, grad_low = layer_grad(1, parts, rstd1, xhat1, out_cotangent, pack1, after=(late1,))
    pieces = gather(grad_low)
    weights1 = weight_grads(
        1, (lefts1, lefts1_other), (rights1, rights1_other), after=(grad_low,)
    )
    big1 = to_pairs(weights1, 0)

    top_keep, top_give = top_parts(gated1, down_w1, after=(weights1[0],))
    top_arrived = paired(top_give, "tensor", 1)

    wide_low0, lift_low0, out_low0, *sends = grad_middle0(
        pieces, wide_pre0, lifted0, down_w0, lift_w0, after=(weights1[0], top_keep)
    )
    parts = scatter(sends)
    rights0, rights0_give = halve(0, (wide_low0, lift_low0, out_low0), after=())
    rights0_other = swap(rights0_give)
    for step in range(1, STEPS):
        weights1 = blocks_join(1, weights1, big1, (rights0,))
        big1 = to_pairs(weights1, step)
    d_scanned0, first0 = adjoint_local(0, parts, pack0, after=(rights0, weights1[0]))
    arrived = line(first0)
    weights0 = weight_grads(
        0, (lefts0, lefts0_other), (rights0, rights0_other), after=(first0,)
    )
    big0 = to_pairs(weights0, 0)
    incoming0, narrow_low0 = adjoint(
        0, d_scanned0, narrow_pre0, arrived, pack0, after=(weights0[0], *big1)
    )
    sends = grad_normed(
        0, wide_low0, narrow_low0, xhat0, pack0, wide_w0, narrow_w0
    )
    parts = scatter(sends)
    states0 = states_before(0, act0, enter0, pack0, after=(sends[0],))
    (sum1,) = big_sum(1, weights1, big1, (), after=(sends[0],))
    top = paired_sum(1, top_keep, top_give, top_arrived, (hidden, pack1), (sends[0],))
    for step in range(1, STEPS):
        weights0 = blocks_join(0, weights0, big0, (sum1, top[0], states0))
        big0 = to_pairs(weights0, step)
    late, late_give = ssm_grads(
        0,
        act0,
        states0,
        d_scanned0,
        incoming0,
        lefts0,
        narrow_low0,
        pack0,
        (late1,),
        after=(weights0[0],),
    )
    grad, grad_give = layer_grad(
        0, parts, rstd0, xhat0, grad_mid, pack0, after=(late, sum1, top[0])
    )
    grad_other = swap(grad_give)
    small_parts = late_join(late, swap(late_give), grad, grad_other, after=())
    small_parts_in = scatter(small_parts, "dp")
    keep, give = big_sum(0, weights0, big0, (sum1,), after=(small_parts[0],))
    big_other = swap(give)
    *own, input_grad, token = own_columns(keep, grad, grad_other, after=())
    (output,) = layer_output(1, None, top, pack1, after=(token,))
    (
        by_wide,
        by_lift,
        by_down,
        wide_b,
        lift_b,
        down_b,
        by_narrow,
        narrow_b,
        by_decay,
        by_input,
        by_output,
        by_skip,
        gain,
        shift,
        section_output,
    ) = finish(
        own,
        (keep, big_other),
        late_sum(small_parts_in),
        (hidden, hidden_other),
        (output, swap(output)),
    )
    return (
        section_output,
        input_grad,
        gain,
        shift,
        by_wide,
        wide_b,
        by_narrow,
        narrow_b,
        by_decay,
        by_input,
        by_output,
        by_skip,
        by_lift,
        lift_b,
        by_down,
        down_b,
    )


def solution(mesh):
    placed = (
        P(None, "dp", None),
        P(None, "dp", None),
        P(),
        P("section", None),
        P("section", None),
        P("section", None, "tensor"),
        P("section", "tensor"),
        P("section", None, "tensor"),
        P("section", "tensor"),
        P("section", "tensor", None),
        P("section", "tensor", None),
        P("section", "tensor", None),
        P("section", "tensor"),
        P("section", None, "tensor"),
        P("section", "tensor"),
        P("section", "tensor", None),
        P("section", None),
    )
    return jax.shard_map(
        local,
        mesh=mesh,
        in_specs=placed,
        out_specs=(
            P("section", None, "dp", "tensor"),
            P("section", None, "dp", "tensor"),
            P("section", ("tensor", "dp")),
            P("section", ("tensor", "dp")),
            P("section", "dp", "tensor"),
            P("section", ("tensor", "dp")),
            P("section", "dp", "tensor"),
            P("section", ("tensor", "dp")),
            P("section", ("tensor", "dp"), None),
            P("section", ("tensor", "dp"), None),
            P("section", ("tensor", "dp"), None),
            P("section", ("tensor", "dp")),
            P("section", "dp", "tensor"),
            P("section", ("tensor", "dp")),
            P("section", ("tensor", "dp"), None),
            P("section", "dp"),
        ),
        check_vma=False,
    )
```

```python
from functools import partial

import jax
import jax.numpy as jnp
from jax import lax
from jax.experimental import pallas as pl
from jax.experimental.pallas import tpu as pltpu
from jax.sharding import PartitionSpec as P

F32, BF16 = jnp.float32, jnp.bfloat16
NORM_EPSILON = 1e-05
LANES = 128
GELU_SCALE, GELU_CUBE = 0.7978845608028654, 0.044715
GAIN, SHIFT, DOWN_B, WIDE_B, LIFT_B, NARROW_B, SKIP = 0, 8, 16, 24, 30, 36, 37
MEGA = 1024 * 1024
SPAN = 40_000_000_000
SEGMENTS = 4
IN_VMEM = pl.BlockSpec(memory_space=pltpu.VMEM)
IN_SMEM = pl.BlockSpec(memory_space=pltpu.SMEM)
IN_PLACE = pl.BlockSpec(memory_space=pl.ANY)
IN_HBM = pl.BlockSpec(memory_space=pltpu.HBM)


def mm(left, right):
    return jnp.dot(left, right, preferred_element_type=F32)


def mm_last(left, right):
    return lax.dot_general(left, right, (((1,), (1,)), ((), ())), preferred_element_type=F32)


def mm_first(left, right, precision=None):
    return lax.dot_general(
        left, right, (((0,), (0,)), ((), ())), preferred_element_type=F32, precision=precision
    )


def gelu(z):
    return 0.5 * z * (1.0 + jnp.tanh(GELU_SCALE * (z + GELU_CUBE * z * z * z)))


def gelu_slope(z):
    square = z * z
    bend = jnp.tanh(GELU_SCALE * (z + GELU_CUBE * z * square))
    return 0.5 * (1.0 + bend) + 0.5 * z * (1.0 - bend * bend) * GELU_SCALE * (
        1.0 + 3.0 * GELU_CUBE * square
    )


class Kernel:
    def __init__(self, lengths, length, layer):
        self.lengths, self.length, self.layer = lengths, length, layer

    def __call__(
        self, name, body, outs, vin=(), places=(), picked=(), scratch=(), after=(), spare=6, span=1, keep=False, direct=(), onto=0
    ):
        n_v, n_a, n_p, n_o, n_s = len(vin), len(places), len(picked), len(outs), len(scratch)
        n_w, n_k = len(after), len(picked) if keep else 0
        layer = self.layer

        def run(*refs):
            k = KernelRefs()
            k.meta = placing(refs[0], self.length)
            at = 1
            k.vin = refs[at : at + n_v]
            at += n_v
            k.places = refs[at : at + n_a]
            at += n_a
            pairs = refs[at : at + 2 * n_p]
            at += 2 * n_p + n_w
            k.outs = refs[at : at + n_o]
            at += n_o
            buffers = refs[at : at + n_k]
            at += n_k
            k.scratch = refs[at : at + n_s]
            at += n_s
            if not keep:
                buffers = refs[at : at + n_p]
                at += n_p
            if n_p:
                sems = refs[at]
                mine = k.meta[0] == layer

                def fetch(source):
                    for i in range(n_p):
                        pltpu.make_async_copy(pairs[2 * i + source], buffers[i], sems.at[i]).start()

                pl.when(mine)(partial(fetch, 0))
                pl.when(jnp.logical_not(mine))(partial(fetch, 1))

                def get(i):
                    pltpu.make_async_copy(pairs[2 * i], buffers[i], sems.at[i]).wait()
                    return buffers[i]

                k.get = get
            body(k)

        extra = [] if keep else [pltpu.VMEM(own.shape, own.dtype) for own, _ in picked]
        if n_p:
            extra.append(pltpu.SemaphoreType.DMA((n_p,)))
        held = sum(
            _size(ref.shape) * ref.dtype.itemsize
            for ref in (*scratch, *extra)
            if ref.memory_space == pltpu.VMEM
        )
        flat = [part for pair in picked for part in pair]
        operands = (self.lengths, *vin, *places, *flat, *after)
        return pl.pallas_call(
            run,
            out_shape=[jax.ShapeDtypeStruct(s, d) for s, d in outs]
            + [jax.ShapeDtypeStruct(own.shape, own.dtype) for own, _ in picked[:n_k]],
            in_specs=[IN_SMEM]
            + [IN_VMEM] * n_v
            + [IN_PLACE] * n_a
            + [IN_HBM] * (2 * n_p)
            + [IN_PLACE] * n_w,
            out_specs=[IN_PLACE if i in direct else IN_VMEM for i in range(n_o + n_k)],
            input_output_aliases={1 + n_v + i: i for i in range(onto)},
            scratch_shapes=[*scratch, *extra],
            compiler_params=pltpu.CompilerParams(vmem_limit_bytes=held + spare * MEGA),
            cost_estimate=pl.CostEstimate(flops=span, bytes_accessed=1, transcendentals=0),
            name=name,
        )(*operands)


class KernelRefs:
    pass


def placing(lengths, length):
    section, ti, di = (lax.axis_index(axis) for axis in ("section", "tensor", "dp"))
    first = -di * length
    second = first + lengths[section, 0]
    return [section, ti, di, first, second, second + lengths[section, 1]]


def _size(shape):
    total = 1
    for extent in shape:
        total *= extent
    return total


def vec(pack, first, count):
    column = pack.shape[1] - LANES
    rows = [pack[first + i : first + i + 1, column:] for i in range(count)]
    return rows[0] if count == 1 else jnp.concatenate(rows, axis=1)


def tables(pack):
    return [pack[:, i * LANES : (i + 1) * LANES] for i in range(4)]


def start_in(meta, first, count):
    hit = False
    for i in range(3):
        hit = jnp.logical_or(hit, (meta[3 + i] >= first) & (meta[3 + i] < first + count))
    return hit


def keep_at(meta, place):
    return jnp.where(start_in(meta, place, 1), 0.0, 1.0)


BLOCK = 32


def scan_blocks(meta, length, carry, step, backward=False, block=BLOCK):
    blocks = length // block

    def one(i, carry):
        t0 = pl.multiple_of((blocks - 1 - i if backward else i) * block, block)
        return lax.cond(
            start_in(meta, t0, block),
            lambda c: step(t0, c, True),
            lambda c: step(t0, c, False),
            carry,
        )

    return lax.fori_loop(0, blocks, one, carry)


def row_groups(ref, t0, block, backward=False):
    groups = range(0, block, 8)
    for g in reversed(groups) if backward else groups:
        rows = ref[pl.ds(t0 + g, 8), :]
        for j in reversed(range(8)) if backward else range(8):
            yield g + j, rows[j : j + 1, :]


def end_state(meta, ref, decay, length, backward=False):
    span = length // SEGMENTS
    a = jnp.exp(-decay)

    def step(i, carried, masked):
        out = []
        for g, state in enumerate(carried):
            t0 = pl.multiple_of(g * span + i * 8, 8)
            for j, row in row_groups(ref, t0, 8, backward):
                if backward:
                    state = a * (state + row)
                    if masked:
                        state = state * keep_at(meta, t0 + j)
                else:
                    if masked:
                        state = state * keep_at(meta, t0 + j)
                    state = a * state + row
            out.append(state)
        return tuple(out)

    def one(i, carried):
        i = span // 8 - 1 - i if backward else i
        hit = False
        for g in range(SEGMENTS):
            hit = jnp.logical_or(hit, start_in(meta, g * span + i * 8, 8))
        return lax.cond(hit, lambda c: step(i, c, True), lambda c: step(i, c, False), carried)

    zero = jnp.zeros_like(decay)
    ends = lax.fori_loop(0, span // 8, one, (zero,) * SEGMENTS)
    across = jnp.exp(decay * (-float(span)))
    order = range(SEGMENTS)
    total = zero
    for g in reversed(order) if backward else order:
        through = jnp.where(start_in(meta, g * span, span), 0.0, 1.0)
        total = ends[g] + through * across * total
    return total


def one_minus_exp(d):
    series = 1.0
    for k in range(8, 1, -1):
        series = 1.0 - d * (1.0 / k) * series
    return jnp.where(d < 0.25, d * series, 1.0 - jnp.exp(-d))


def crossing(meta, arrived, decay, length, direction):
    total = jnp.zeros_like(decay)
    for s, part in enumerate(arrived):
        apart = direction * (meta[2] - jnp.bitwise_xor(meta[2], s + 1)) - 1
        first = -apart * length if direction == 1 else length
        open_way = jnp.logical_and(apart >= 0, jnp.logical_not(start_in(meta, first, apart * length)))
        reach = jnp.exp(decay * (-float(length)) * jnp.maximum(apart, 0).astype(F32))
        total = total + jnp.where(open_way, reach * part[...], 0.0)
    return total


def local(
    layer_input,
    out_cotangent,
    seq_lengths,
    norm_gain,
    norm_bias,
    wide_weight,
    wide_bias,
    narrow_weight,
    narrow_bias,
    ssm_decay,
    ssm_input,
    ssm_output,
    ssm_skip,
    lift_weight,
    lift_bias,
    down_weight,
    down_bias,
):
    section = lax.axis_index("section")
    nt, nd = lax.axis_size("tensor"), lax.axis_size("dp")
    T, D = layer_input.shape[1], layer_input.shape[2]
    FW = wide_weight.shape[2]
    HC = narrow_weight.shape[2]
    H = lift_weight.shape[1]
    N = ssm_decay.shape[2]
    DC = D // nt
    kernels = [Kernel(seq_lengths, T, 0), Kernel(seq_lengths, T, 1)]

    flip = [(0, 1), (1, 0)]

    def swap(x):
        return lax.ppermute(x, "section", flip)

    def make_pack():
        vectors = (
            (norm_gain, GAIN),
            (norm_bias, SHIFT),
            (down_bias, DOWN_B),
            (wide_bias, WIDE_B),
            (lift_bias, LIFT_B),
            (narrow_bias, NARROW_B),
            (ssm_skip, SKIP),
        )
        sources = [ssm_decay, ssm_input, ssm_output]
        sources = [jnp.swapaxes(part, 1, 2)[0] for part in sources]

        def body(k):
            pack, held, sems = k.outs[0], k.scratch[:-1], k.scratch[-1]
            copies = [
                pltpu.make_async_copy(source, target, sems.at[i])
                for i, (source, target) in enumerate(zip(k.places, held))
            ]
            for copy in copies:
                copy.start()
            column = 4 * LANES
            pack[:, column:] = jnp.zeros((N, LANES), F32)
            for copy in copies:
                copy.wait()
            for i, source in zip((0, 2, 3), held):
                pack[:, i * LANES : (i + 1) * LANES] = source[...]
            pack[:, LANES : 2 * LANES] = one_minus_exp(held[0][...])
            for (source, first), ref in zip(vectors, held[3:]):
                for i in range(source.shape[1] // LANES):
                    pack[first + i : first + i + 1, column:] = ref[
                        :, i * LANES : (i + 1) * LANES
                    ]

        places = (*sources, *(v for v, _ in vectors))
        return kernels[0](
            "make_pack",
            body,
            [((N, 5 * LANES), F32)],
            places=places,
            scratch=[pltpu.VMEM(part.shape, F32) for part in places]
            + [pltpu.SemaphoreType.DMA((len(places),))],
            spare=56,
            span=SPAN,
        )[0]

    pack = make_pack()
    pack_other = swap(pack)
    narrow_w = (narrow_weight[0], swap(narrow_weight[0]))
    wide_w = (wide_weight[0], swap(wide_weight[0]))
    lift_w = (lift_weight[0], swap(lift_weight[0]))
    down_w = (down_weight[0], swap(down_weight[0]))

    def paired(part, axis, s):
        n = lax.axis_size(axis)
        return lax.ppermute(part, axis, [(i, i ^ s) for i in range(n)])

    def scatter(parts, axis="tensor"):
        n = len(parts)
        return (parts[0], *(paired(parts[s], axis, n - s) for s in range(1, n)))

    def gather(part, forward=False):
        if forward and nt == 4:
            across = paired(part, "tensor", 2)
            beside = paired(part, "tensor", 1)
            return (part, beside, across, paired(across, "tensor", 1))
        return (part, *(paired(part, "tensor", s) for s in range(1, nt)))

    def paired_parts(meta, keep, give, part):
        for i in range(nt // 2):
            for bit, out in ((0, keep), (1, give)):
                out[i] = part(jnp.bitwise_xor(meta[1], 2 * i + bit)).astype(out.dtype)

    def paired_outs(width):
        return [((nt // 2, T, width), F32), ((nt // 2, T, width), BF16)]

    def parts_join(layer, keep, arrived, base, after):
        half, width = keep.shape[0] // 2, keep.shape[2]

        def body(k):
            for i in range(2 * half):
                part = k.vin[0][i] + k.vin[1][i].astype(F32)
                if base and i == 0:
                    part = part + k.vin[2][...] + column_rows(k.vin[3], DOWN_B, k.meta[1])
                out = k.outs[i % 2]
                out[i // 2] = part.astype(out.dtype)

        return kernels[layer](
            f"parts_join{layer}",
            body,
            [((half, T, width), F32), ((half, T, width), BF16)],
            vin=(keep, arrived, *base),
            after=after,
        )

    def paired_sum(layer, keep, give, arrived, base, after):
        step = 2
        while step < nt:
            keep, give = parts_join(layer, keep, arrived, base if step == 2 else (), after)
            arrived = paired(give, "tensor", step)
            step *= 2
        return keep, arrived

    def line(value):
        return tuple(paired(value, "dp", s + 1) for s in range(nd - 1))

    def target(mine, s, n):
        return jnp.bitwise_xor(mine, (n - s) % n)

    HALVES = (FW // 2, FW // 2, D // 2)
    RIGHT = sum(HALVES)

    def turn(layer, sources, after):
        def body(k):
            row = 0
            for source in k.vin:
                for c in range(0, source.shape[1], 256):
                    block = source[:, c : c + 256].astype(F32)
                    k.outs[0][row : row + 256, :] = jnp.transpose(block).astype(BF16)
                    row += 256

        height = sum(part.shape[1] for part in sources)
        return kernels[layer](f"turn{layer}", body, [((height, T), BF16)], vin=sources, after=after)[0]

    def halve(layer, sources, after):
        def body(k):
            at = 0
            for source, width in zip(k.vin, HALVES):
                for out, which in zip(k.outs, (k.meta[0], 1 - k.meta[0])):
                    here = pl.ds(pl.multiple_of(which * width, LANES), width)
                    out[:, at : at + width] = source[:, here]
                at += width

        return kernels[layer](
            f"halve{layer}", body, [((T, RIGHT), BF16)] * 2, vin=sources, after=after
        )

    def choose(layer, pairs, after):
        def body(k):
            for i in range(len(pairs)):
                k.get(i)

        return kernels[layer](f"choose{layer}", body, [], picked=pairs, after=after, keep=True, spare=30)

    def norm_rows(rows, emit):
        def block(i, _):
            here = pl.ds(pl.multiple_of(i * 32, 32), 32)
            x = rows[here, :].astype(F32)
            offset = x - jnp.mean(x, axis=1, keepdims=True)
            spread = jnp.mean(offset * offset, axis=1, keepdims=True)
            inverse = lax.rsqrt(spread + NORM_EPSILON)
            emit(here, offset * inverse, inverse)
            return 0

        lax.fori_loop(0, T // 32, block, 0, unroll=4)

    def norm0(after):
        def body(k):
            xhat, rstd = k.outs
            rows, sems = k.scratch
            copy = pltpu.make_async_copy(k.places[0].at[k.meta[0]], rows, sems.at[0])
            copy.start()
            copy.wait()

            def emit(here, standard, inverse):
                xhat[here, :] = standard
                rstd[here, :] = jnp.broadcast_to(inverse, (32, LANES))

            norm_rows(rows, emit)

        return kernels[0](
            "norm0",
            body,
            [((T, D), F32), ((T, LANES), F32)],
            places=(layer_input,),
            after=after,
            scratch=[pltpu.VMEM((T, D), BF16), pltpu.SemaphoreType.DMA((1,))],
            span=SPAN,
        )

    def front(layer, source, pack, narrow, after=()):
        def body(k):
            meta = k.meta
            normed, narrow_pre, act, final = k.outs[:4]
            if layer == 0:
                pk, upper = k.outs[4:]
                keep_or_give(meta, pk, upper, k.vin[1][...], k.vin[2][...], False)
            else:
                xhat, rstd = k.outs[4:]
                rows = k.scratch[0]
                assemble(meta, k.vin, rows)
                pk, weight = k.vin[nt:]
            gain, shift = vec(pk, GAIN, D // LANES), vec(pk, SHIFT, D // LANES)
            if layer == 0:
                for r in range(0, T, 32):
                    here = slice(r, r + 32)
                    normed[here, :] = (k.vin[0][here, :] * gain + shift).astype(BF16)
                weight = k.get(0)
            else:

                def emit(here, standard, inverse):
                    xhat[here, :] = standard
                    rstd[here, :] = jnp.broadcast_to(inverse, (32, LANES))
                    normed[here, :] = (standard * gain + shift).astype(BF16)

                norm_rows(rows, emit)
            pre = mm(normed[...], weight[...]) + vec(pk, NARROW_B, 1)
            narrow_pre[...] = pre
            act[...] = gelu(pre)
            final[...] = end_state(meta, act, tables(pk)[0], T)

        return kernels[layer](
            f"front{layer}",
            body,
            [((T, D), BF16), ((T, HC), F32), ((T, HC), F32), ((N, HC), F32)]
            + (
                [(pack[0].shape, F32)] * 2
                if layer == 0
                else [((T, D), F32), ((T, LANES), F32)]
            ),
            after=after,
            vin=(source, *pack) if layer == 0 else (*source, pack, narrow),
            picked=(narrow,) if layer == 0 else (),
            keep=True,
            scratch=[] if layer == 0 else [pltpu.VMEM((T, D), BF16)],
            span=SPAN,
        )

    def wide0(normed, pack):
        def body(k):
            bias = vec(k.vin[1], WIDE_B, FW // LANES)
            weight = k.get(0)
            for c in range(0, FW, 256):
                k.outs[0][:, c : c + 256] = (
                    mm(k.vin[0][...], weight[:, c : c + 256]) + bias[:, c : c + 256]
                )

        return kernels[0](
            "wide0",
            body,
            [((T, FW), F32)],
            vin=(normed, pack),
            picked=(wide_w,),
            keep=True,
            spare=6,
        )

    def wide1(normed, d_gated, pack, wide, lift, after):
        def body(k):
            wide_pre, lift_low = k.outs[:2]
            pk, weight, lift = k.vin[2:]
            bias = vec(pk, WIDE_B, FW // LANES)
            for c in range(0, FW, 256):
                pre = mm(k.vin[0][...], weight[:, c : c + 256]) + bias[:, c : c + 256]
                wide_pre[:, c : c + 256] = pre
                lift_low[:, c : c + 256] = (k.vin[1][:, c : c + 256] * gelu(pre)).astype(BF16)
            lift_parts(k.meta, lift_low, lift, k.outs[2:])

        return kernels[1](
            "wide1",
            body,
            [((T, FW), F32), ((T, FW), BF16)] + parted(HC),
            vin=(normed, d_gated, pack, wide, lift),
            after=after,
            span=SPAN,
        )

    def parted(width, rows=T):
        return [((rows, width), F32)] + [((rows, width), BF16)] * (nt - 1)

    def lift_parts(meta, lift_low, lift, sends):
        for s in range(nt):
            at = target(meta[1], s, nt) * HC
            part = mm_last(lift_low[...], lift[pl.ds(pl.multiple_of(at, HC), HC), :])
            sends[s][...] = part.astype(sends[s].dtype)

    def carry(layer, act, arrived, pack, after=()):
        def body(k):
            meta = k.meta
            u = k.vin[0]
            entering, scanned = k.outs
            local_out = k.scratch[0]
            pk = k.vin[1]
            decay, grown, rate_in, read_out = tables(pk)
            skip = vec(pk, SKIP, 1)
            a, read = jnp.exp(-decay), read_out * rate_in * grown
            state = crossing(meta, k.vin[2:], decay, T, 1)
            entering[...] = state

            def step(t0, state, masked):
                outs = []
                for j, row in row_groups(u, t0, BLOCK):
                    if masked:
                        state = state * keep_at(meta, t0 + j)
                    state = a * state + row
                    outs.append(jnp.sum(read * state, axis=0, keepdims=True) + skip * row)
                for g in range(0, BLOCK, 8):
                    local_out[pl.ds(t0 + g, 8), :] = jnp.concatenate(outs[g : g + 8], axis=0)
                return state

            scan_blocks(meta, T, state, step)
            scanned[...] = local_out[...].astype(BF16)

        return kernels[layer](
            f"carry{layer}",
            body,
            [((N, HC), F32), ((T, HC), BF16)],
            vin=(act, pack, *arrived),
            after=after,
            scratch=[pltpu.VMEM((T, HC), F32)],
            span=SPAN,
        )

    def assemble(meta, parts, whole):
        width = parts[0].shape[1]
        for s in range(nt):
            at = jnp.bitwise_xor(meta[1], s) * width
            whole[:, pl.ds(pl.multiple_of(at, width), width)] = parts[s][...]

    def down_parts(meta, gated, down, sends):
        for s in range(nt):
            at = target(meta[1], s, nt) * DC
            part = mm(gated[...], down[:, pl.ds(pl.multiple_of(at, DC), DC)])
            sends[s][...] = part.astype(sends[s].dtype)

    def middle0(pieces, wide_pre, pack, lift, down):
        def body(k):
            scanned, lifted, gated = k.outs[:3]
            assemble(k.meta, k.vin[:nt], scanned)
            wide_pre, pk, lift, down = k.vin[nt:]
            bias = vec(pk, LIFT_B, FW // LANES)
            for c in range(0, FW, 256):
                part = mm(scanned[...], lift[:, c : c + 256]) + bias[:, c : c + 256]
                lifted[:, c : c + 256] = part
                gated[:, c : c + 256] = (part * gelu(wide_pre[:, c : c + 256])).astype(BF16)
            down_parts(k.meta, gated, down, k.outs[3:])

        return kernels[0](
            "middle0",
            body,
            [((T, H), BF16), ((T, FW), F32), ((T, FW), BF16)] + parted(DC),
            vin=(*pieces, wide_pre, pack, lift, down),
            span=SPAN,
        )

    def middle1(pieces, wide_pre, d_gated, pack, lift):
        def body(k):
            scanned, gated, wide_low = k.outs
            assemble(k.meta, k.vin[:nt], scanned)
            pre, grad, pk, lift = k.vin[nt:]
            bias = vec(pk, LIFT_B, FW // LANES)
            for c in range(0, FW, 256):
                part = mm(scanned[...], lift[:, c : c + 256]) + bias[:, c : c + 256]
                z = pre[:, c : c + 256]
                gated[:, c : c + 256] = (part * gelu(z)).astype(BF16)
                wide_low[:, c : c + 256] = (grad[:, c : c + 256] * part * gelu_slope(z)).astype(BF16)

        return kernels[1](
            "middle1",
            body,
            [((T, H), BF16), ((T, FW), BF16), ((T, FW), BF16)],
            vin=(*pieces, wide_pre, d_gated, pack, lift),
            span=SPAN,
        )

    def top_parts(gated, down, after):
        def body(k):
            gated, down = k.vin
            paired_parts(
                k.meta,
                *k.outs,
                lambda at: mm(gated[...], down[:, pl.ds(pl.multiple_of(at * DC, DC), DC)]),
            )

        return kernels[1]("top_parts", body, paired_outs(DC), vin=(gated, down), after=after)

    def column_rows(pk, first, at):
        per = DC // LANES
        best = vec(pk, first, per)
        for i in range(1, nt):
            best = jnp.where(at == i, vec(pk, first + i * per, per), best)
        return best

    def keep_or_give(meta, keep, give, first, second, by_layer=True):
        lower = meta[0] == 0
        keep[...] = jnp.where(lower, first, second)
        give[...] = jnp.where(lower, second, first)

    def layer_output(layer, before, parts, pack, after=()):
        def body(k):
            meta = k.meta
            if layer == 0:
                rows = k.scratch[0]
                copy = pltpu.make_async_copy(
                    k.places[0].at[meta[0], :, pl.ds(pl.multiple_of(meta[1] * DC, DC), DC)],
                    rows,
                    k.scratch[1].at[0],
                )
                copy.start()
                copy.wait()
                total = rows[...].astype(F32)
                for part in k.vin[1:]:
                    total = total + part[...].astype(F32)
                total = total + column_rows(k.vin[0], DOWN_B, meta[1])
            else:
                total = k.vin[1][0] + k.vin[2][0].astype(F32)
            if layer == 0:
                k.outs[0][...] = total
                k.outs[1][...] = total.astype(BF16)
            else:
                k.outs[0][...] = total

        return kernels[layer](
            f"layer_output{layer}",
            body,
            [((T, DC), F32)] + ([((T, DC), BF16)] if layer == 0 else []),
            vin=(pack, *parts),
            after=after,
            places=(before,) if layer == 0 else (),
            scratch=[pltpu.VMEM((T, DC), BF16), pltpu.SemaphoreType.DMA((1,))] if layer == 0 else [],
            span=1 if layer else SPAN,
        )

    def grad_gated1(down, after):
        def body(k):
            rows = k.outs[1]
            copy = pltpu.make_async_copy(k.places[0].at[k.meta[0]], rows, k.scratch[0].at[0])
            copy.start()
            copy.wait()
            down = k.vin[0]
            for c in range(0, FW, 256):
                k.outs[0][:, c : c + 256] = mm_last(rows[...], down[c : c + 256, :])

        return kernels[1](
            "grad_gated1",
            body,
            [((T, FW), F32), ((T, D), BF16)],
            places=(out_cotangent,),
            vin=(down,),
            after=after,
            scratch=[pltpu.SemaphoreType.DMA((1,))],
        )

    def grad_middle0(pieces, wide_pre, lifted, down, lift, after=()):
        def body(k):
            wide_low, low, rows = k.outs[:3]
            pre, raised, down, lift = k.vin[nt:]
            assemble(k.meta, k.vin[:nt], rows)
            for c in range(0, FW, 256):
                grad = mm_last(rows[...], down[c : c + 256, :])
                z = pre[:, c : c + 256]
                low[:, c : c + 256] = (grad * gelu(z)).astype(BF16)
                wide_low[:, c : c + 256] = (
                    grad * raised[:, c : c + 256] * gelu_slope(z)
                ).astype(BF16)
            lift_parts(k.meta, low, lift, k.outs[3:])

        return kernels[0](
            "grad_middle0",
            body,
            [((T, FW), BF16), ((T, FW), BF16), ((T, D), BF16)] + parted(HC),
            vin=(*pieces, wide_pre, lifted, down, lift),
            after=after,
            span=SPAN,
        )

    def adjoint_local(layer, parts, pack, after=()):
        def body(k):
            grads, first = k.outs
            total = k.vin[1][...]
            for part in k.vin[2:]:
                total = total + part[...].astype(F32)
            grads[...] = total
            first[...] = end_state(k.meta, grads, tables(k.vin[0])[0], T, backward=True)

        return kernels[layer](
            f"adjoint_local{layer}",
            body,
            [((T, HC), F32), ((N, HC), F32)],
            vin=(pack, *parts),
            after=after,
            span=SPAN,
        )

    def adjoint(layer, d_scanned, narrow_pre, arrived, pack, after=()):
        def body(k):
            meta = k.meta
            grads, pre, pk = k.vin[:3]
            after, narrow_low = k.outs
            d_narrow = k.scratch[0]
            decay, grown, rate_in, read_out = tables(pk)
            skip = vec(pk, SKIP, 1)
            a, read = jnp.exp(-decay), read_out * rate_in * grown
            incoming = crossing(meta, k.vin[3:], decay, T, -1)
            after[...] = incoming

            def step(t0, z, masked):
                outs = [None] * BLOCK
                for j, row in row_groups(grads, t0, BLOCK, True):
                    w = z + row
                    outs[j] = jnp.sum(read * w, axis=0, keepdims=True) + skip * row
                    z = a * w
                    if masked:
                        z = z * keep_at(meta, t0 + j)
                for g in range(0, BLOCK, 8):
                    d_narrow[pl.ds(t0 + g, 8), :] = jnp.concatenate(outs[g : g + 8], axis=0)
                return z

            scan_blocks(meta, T, incoming, step, backward=True)
            narrow_low[...] = (d_narrow[...] * gelu_slope(pre[...])).astype(BF16)

        return kernels[layer](
            f"adjoint{layer}",
            body,
            [((N, HC), F32), ((T, HC), BF16)],
            vin=(d_scanned, narrow_pre, pack, *arrived),
            after=after,
            scratch=[pltpu.VMEM((T, HC), F32)],
            span=SPAN,
        )

    LATE = D // 2 + 2 * N

    def states_before(layer, act, entering, pack, after):
        def body(k):
            u, enter, pk = k.vin
            a = jnp.exp(-tables(pk)[0])

            def ahead(t0, state, masked):
                for j, row in row_groups(u, t0, BLOCK):
                    if masked:
                        state = state * keep_at(k.meta, t0 + j)
                    k.outs[0][t0 + j] = state
                    state = a * state + row
                return state

            scan_blocks(k.meta, T, enter[...], ahead)

        return kernels[layer](
            f"states_before{layer}",
            body,
            [((T, N, HC), F32)],
            vin=(act, entering, pack),
            after=after,
        )[0]

    def ssm_grads(layer, act, states, d_scanned, incoming, turned, narrow_low, pack, upper, after):
        def body(k):
            meta = k.meta
            u, states, grads, incoming, low, pk = k.vin[:6]
            lefts, sems = k.scratch[:2]
            late = k.outs[0] if layer == 1 else k.scratch[2]
            copy = pltpu.make_async_copy(k.places[0].at[0:D, :], lefts, sems.at[0])
            copy.start()
            decay, grown, rate_in, read_out = tables(pk)
            a = jnp.exp(-decay)
            zero = jnp.zeros((N, HC), F32)

            def back(t0, carried, masked):
                z, with_rows, with_states = carried
                rows = row_groups(u, t0, BLOCK, True)
                for (j, row), (_, grad) in zip(rows, row_groups(grads, t0, BLOCK, True)):
                    w = z + grad
                    with_rows = with_rows + w * row
                    with_states = with_states + w * states[t0 + j]
                    z = a * w
                    if masked:
                        z = z * keep_at(meta, t0 + j)
                return z, with_rows, with_states

            _, with_rows, with_states = scan_blocks(
                meta, T, (incoming[...], zero, zero), back, backward=True
            )
            b = rate_in * grown
            first, second = slice(D // 2, D // 2 + N), slice(D // 2 + N, D // 2 + 2 * N)
            late[first, 0:LANES] = a * read_out * (rate_in * with_rows - b * with_states)
            late[first, LANES:] = grown * read_out * with_rows
            late[second, 0:LANES] = b * with_rows
            late[second, LANES:] = zero
            row = D // 2 + N
            late[row : row + 1, LANES:] = jnp.sum(low[...].astype(F32), axis=0, keepdims=True)
            late[row + 1 : row + 2, LANES:] = jnp.sum(u[...] * grads[...], axis=0, keepdims=True)
            copy.wait()
            for h in range(2):
                late[0 : D // 2, h * LANES : (h + 1) * LANES] = mm(
                    lefts[h * (D // 2) : (h + 1) * (D // 2), :], low[...]
                )
            if layer == 0:
                keep_or_give(meta, k.outs[0], k.outs[1], late[...], k.vin[6][...])

        return kernels[layer](
            f"ssm_grads{layer}",
            body,
            [((LATE, 2 * LANES), F32)] * (2 - layer),
            vin=(act, states, d_scanned, incoming, narrow_low, pack, *upper),
            places=(turned,),
            span=1 if layer else SPAN,
            after=after,
            scratch=[
                pltpu.VMEM((D, T), BF16),
                pltpu.SemaphoreType.DMA((1,)),
            ]
            + ([pltpu.VMEM((LATE, 2 * LANES), F32)] if layer == 0 else []),
        )

    def grad_normed(layer, wide_low, narrow_low, xhat, pack, wide, narrow, after=()):
        def body(k):
            meta = k.meta
            wide_low, narrow_in, standard, gains, wide, narrow = k.vin
            ones = jnp.ones((8, DC), BF16)
            sums = jnp.zeros((16, T), F32)
            for s in range(nt):
                at = target(meta[1], s, nt)
                here = pl.ds(pl.multiple_of(at * DC, DC), DC)
                part = mm_last(wide_low[...], wide[here, :]) + mm_last(
                    narrow_in[...], narrow[here, :]
                )
                scaled = part * column_rows(gains, GAIN, at)
                with_x = scaled * standard[:, here]
                sums = sums + jnp.concatenate(
                    [mm_last(ones, scaled.astype(BF16)), mm_last(ones, with_x.astype(BF16))], axis=0
                )
                k.outs[s][0:T, :] = part.astype(k.outs[s].dtype)
            for s in range(nt):
                k.outs[s][T:, :] = sums.astype(k.outs[s].dtype)

        return kernels[layer](
            f"grad_normed{layer}",
            body,
            parted(DC, T + 16),
            vin=(wide_low, narrow_low, xhat, pack, wide, narrow),
            after=after,
            span=SPAN,
        )

    def layer_grad(layer, parts, rstd, xhat, grad_out, pack, after):
        def body(k):
            meta = k.meta
            here = pl.ds(pl.multiple_of(meta[1] * DC, DC), DC)
            standard, sems = k.scratch[0], k.scratch[1]
            copy = pltpu.make_async_copy(k.places[0].at[:, here], standard, sems.at[0])
            copy.start()
            if layer == 1:
                copy_out = pltpu.make_async_copy(
                    k.places[1].at[meta[0], :, here], k.scratch[2], sems.at[1]
                )
                copy_out.start()
            total, sums = k.vin[0][0:T, :], k.vin[0][T:, :]
            for part in k.vin[1:nt]:
                total = total + part[0:T, :].astype(F32)
                sums = sums + part[T:, :].astype(F32)
            inverse = k.vin[nt]
            row = lax.broadcasted_iota(jnp.int32, (16, LANES), 0)
            first = mm_first(sums, (row == 0).astype(F32), lax.Precision.HIGHEST) * (1.0 / D)
            second = mm_first(sums, (row == 8).astype(F32), lax.Precision.HIGHEST) * (1.0 / D)
            scaled = total * column_rows(k.vin[nt + 1], GAIN, meta[1])
            copy.wait()
            if layer == 1:
                copy_out.wait()
                grad_in = k.scratch[2][...].astype(F32)
            else:
                grad_in = k.vin[nt + 2][...]
            if layer == 1:
                result = k.outs[0]
            else:
                keep, give, upper = k.outs[0], k.outs[1], k.vin[nt + 2]
                result = k.scratch[2]
            for c in range(0, DC, LANES):
                x = standard[:, c : c + LANES]
                grad = grad_in[0:T, c : c + LANES] + inverse[...] * (
                    scaled[:, c : c + LANES] - first - x * second
                )
                result[0:T, c : c + LANES] = grad
                if layer == 1:
                    k.outs[1][:, c : c + LANES] = grad.astype(BF16)
            result[T:, :] = jnp.zeros((8, DC), F32)
            result[T : T + 1, :] = jnp.sum(total * standard[...], axis=0, keepdims=True)
            result[T + 1 : T + 2, :] = jnp.sum(total, axis=0, keepdims=True)
            if layer == 0:
                lower = meta[0] == 0
                keep[...] = jnp.where(lower, result[...], upper[...])
                give[0:T, :] = jnp.where(lower, upper[0:T, :], result[0:T, :]).astype(BF16)
                sums = jnp.where(lower, upper[T:, :], result[T:, :])
                sums = jnp.concatenate([sums, jnp.zeros((8, DC), F32)], axis=0)
                give[T:, :] = sums.astype(BF16)

        return kernels[layer](
            f"layer_grad{layer}",
            body,
            [((T + 8, DC), F32), ((T, DC), BF16)]
            if layer == 1
            else [((T + 8, DC), F32), ((T + 16, DC), BF16)],
            after=after,
            vin=(*parts, rstd, pack) + (() if layer == 1 else (grad_out,)),
            places=(xhat,) + ((grad_out,) if layer == 1 else ()),
            scratch=[pltpu.VMEM((T, DC), F32), pltpu.SemaphoreType.DMA((2,))]
            + [pltpu.VMEM((T, DC), BF16) if layer == 1 else pltpu.VMEM((T + 8, DC), F32)],
            span=SPAN,
        )

    RW, RL, RD = D // nd, H // nd, FW // nd
    CW, CD = HALVES[0] // LANES, HALVES[2] // LANES
    AT_L = RW * CW
    AT_D = AT_L + RL * CW
    AT_V = AT_D + RD * CD
    BIG = AT_V + 16
    CUT = AT_L + 2 * RL
    STEPS = nd.bit_length() - 1

    def mirrored(s):
        return sum(((s >> b) & 1) << (STEPS - 1 - b) for b in range(STEPS))

    def block_outs(count):
        return [((count, rows, LANES), BF16) for rows in (CUT, BIG - CUT) for _ in range(2)]

    def to_pairs(blocks, step):
        return (
            paired(blocks[1], "dp", 1 << step),
            paired(blocks[3], "dp", 1 << (STEPS - 1 - step)),
        )

    def blocks_join(layer, blocks, arrived, after):
        count = blocks[0].shape[0] // 2

        def body(k):
            for h in range(2):
                for i in range(2 * count):
                    part = k.vin[2 * h][i].astype(F32) + k.vin[2 * h + 1][i].astype(F32)
                    k.outs[2 * h + i % 2][i // 2] = part.astype(BF16)

        return kernels[layer](
            f"blocks_join{layer}",
            body,
            block_outs(count),
            vin=(blocks[0], arrived[0], blocks[2], arrived[1]),
            after=after,
        )

    def put(k, s, row, value):
        first = row < CUT
        i = s if first else mirrored(s)
        out = k.outs[i % 2 if first else 2 + i % 2]
        row -= 0 if first else CUT
        out[i // 2, row : row + value.shape[0], :] = value.astype(BF16)

    def weight_grads(layer, lefts, rights, after):
        def body(k):
            meta = k.meta
            left, right = k.vin[:2], k.vin[2:]

            def product(row, rows, at, width, at_row):
                columns = slice(at, at + width)
                for s in range(nd):
                    first = row + jnp.bitwise_xor(meta[2], s) * rows
                    here = pl.ds(pl.multiple_of(first, 16), rows)
                    part = mm(left[0][here, :], right[0][:, columns])
                    part = part + mm(left[1][here, :], right[1][:, columns])
                    for h in range(0, width, LANES):
                        put(k, s, at_row + h // LANES * rows, part[:, h : h + LANES])

            product(0, RW, 0, HALVES[0], 0)
            product(D, RL, HALVES[0], HALVES[1], AT_L)
            product(D + H, RD, HALVES[0] + HALVES[1], HALVES[2], AT_D)
            sums = k.scratch[0]
            sums[...] = jnp.zeros((16, LANES), F32)
            for i in range(RIGHT // LANES):
                here = slice(i * LANES, (i + 1) * LANES)
                total = jnp.sum(right[0][:, here].astype(F32), axis=0, keepdims=True)
                total = total + jnp.sum(right[1][:, here].astype(F32), axis=0, keepdims=True)
                sums[i : i + 1, :] = total
            for s in range(nd):
                put(k, s, AT_V, sums[...])

        return kernels[layer](
            f"weight_grads{layer}",
            body,
            block_outs(nd // 2),
            vin=(*lefts, *rights),
            after=after,
            scratch=[pltpu.VMEM((16, LANES), F32)],
        )

    SMALL = RW + 3 * N + 16

    def late_join(keep, other, grad, grad_other, after):
        def body(k):
            meta = k.meta
            own, other, grad, grad_other = k.vin
            rest = k.scratch[0]

            def summed(rows, columns):
                return own[rows, columns] + other[rows, columns]

            half = D // 2
            left, right = slice(0, LANES), slice(LANES, 2 * LANES)
            upper = slice(half, half + N)
            rest[0:N, :] = summed(upper, left)
            rest[N : 2 * N, :] = summed(upper, right)
            rest[2 * N : 3 * N, :] = summed(slice(half + N, half + 2 * N), left)
            rest[3 * N : 3 * N + 8, :] = summed(slice(half + N, half + N + 8), right)
            rest[3 * N + 8 :, :] = jnp.zeros((8, LANES), F32)
            per = DC // LANES
            for i in range(2):
                row = grad[T + i : T + i + 1, :] + grad_other[T : T + 16, :].astype(F32)[i : i + 1, :]
                for h in range(per):
                    first = 3 * N + 8 + i * per + h
                    rest[first : first + 1, :] = row[:, h * LANES : (h + 1) * LANES]
            for s in range(nd):
                at = target(meta[2], s, nd) * RW
                here = pl.ds(pl.multiple_of(lax.rem(at, half), 16), RW)
                for h in range(2):

                    def put(h=h, out=k.outs[s]):
                        columns = slice(h * LANES, (h + 1) * LANES)
                        out[0:RW, :] = summed(here, columns).astype(BF16)

                    pl.when(at // half == h)(put)
                k.outs[s][RW:, :] = rest[...].astype(BF16)

        return kernels[0](
            "late_join",
            body,
            [((SMALL, LANES), BF16)] * nd,
            vin=(keep, other, grad, grad_other),
            after=after,
            scratch=[pltpu.VMEM((3 * N + 16, LANES), F32)],
        )

    def pick(meta, flat, out):
        width = out.shape[1]
        best = flat[:, 0:width]
        for i in range(1, nd):
            best = jnp.where(meta[2] == i, flat[:, i * width : (i + 1) * width], best)
        out[...] = best

    def chunk(meta, source, first, count, out):
        flat = [source[first + i : first + i + 1, :] for i in range(count)]
        pick(meta, flat[0] if count == 1 else jnp.concatenate(flat, axis=1), out)

    def big_sum(layer, blocks, arrived, upper, after):
        def body(k):
            for h, (first, rows) in enumerate(((0, CUT), (CUT, BIG - CUT))):
                for r in range(0, rows, 256):
                    inner = slice(r, min(r + 256, rows))
                    here = slice(first + inner.start, first + inner.stop)
                    total = k.vin[2 * h][0, inner, :].astype(F32)
                    total = total + k.vin[2 * h + 1][0, inner, :].astype(F32)
                    if layer == 1:
                        k.outs[0][here, :] = total
                    else:
                        lower = k.meta[0] == 0
                        other = k.vin[4][here, :]
                        k.outs[0][here, :] = jnp.where(lower, total, other)
                        k.outs[1][here, :] = jnp.where(lower, other, total).astype(BF16)

        return kernels[layer](
            f"big_sum{layer}",
            body,
            [((BIG, LANES), F32)] + ([((BIG, LANES), BF16)] if layer == 0 else []),
            vin=(blocks[0], arrived[0], blocks[2], arrived[1], *upper),
            after=after,
        )

    def late_sum(parts):
        def body(k):
            total = k.vin[0][...].astype(F32)
            for part in k.vin[1:]:
                total = total + part[...].astype(F32)
            k.outs[0][...] = total

        return kernels[0]("late_sum", body, [((SMALL, LANES), F32)], vin=parts, span=SPAN)[0]

    def big_places():
        return ((0, RW, CW), (AT_L, RL, CW), (AT_D, RD, CD))

    def own_columns(keep, grad, grad_other, after):
        def body(k):
            meta = k.meta
            *outs, grads, token = k.outs
            token[...] = jnp.zeros((8, LANES), F32)
            rows, sems = k.scratch
            rows[...] = k.vin[0][0:T, :].astype(F32)
            moves = [(k.places[1].at[0:T, :], grads.at[0, meta[0]]), (rows, grads.at[0, 1 - meta[0]])]
            for out, (first, height, columns) in zip(outs, big_places()):
                for c in range(columns):
                    at = pl.multiple_of((meta[0] * columns + c) * LANES, LANES)
                    moves.append(
                        (
                            k.places[0].at[first + c * height : first + (c + 1) * height, :],
                            out.at[0, :, pl.ds(at, LANES)],
                        )
                    )
            moves = [
                pltpu.make_async_copy(source, out, sems.at[i])
                for i, (source, out) in enumerate(moves)
            ]
            for move in moves:
                move.start()
            for move in moves:
                move.wait()

        return kernels[0](
            "own_columns",
            body,
            [
                ((1, RW, FW), F32),
                ((1, RL, FW), F32),
                ((1, RD, D), F32),
                ((1, 2, T, DC), F32),
                ((8, LANES), F32),
            ],
            vin=(grad_other,),
            places=(keep, grad),
            after=after,
            direct=(0, 1, 2, 3),
            scratch=[pltpu.VMEM((T, DC), F32), pltpu.SemaphoreType.DMA((2 + 2 * CW + CD,))],
        )

    def finish(own, big, small, lower, upper):
        def body(k):
            meta = k.meta
            wide, lift, down, rows, turned, sems = k.scratch
            by_wide, by_lift, by_down = k.outs[:3]
            wide_b, lift_b, down_b = k.outs[3:6]
            by_narrow, narrow_b, *by_ssm, by_skip, gain, shift, outputs = k.outs[6:]
            keep, give, late = k.vin

            def output(layer, i):
                return pltpu.make_async_copy(
                    k.places[3 + 2 * layer + i],
                    outputs.at[0, meta[0] if i == 0 else 1 - meta[0]],
                    sems.at[3 + i],
                )

            def send(layer):
                for i in range(2):
                    output(layer, i).start()

            pl.when(meta[0] == 0)(partial(send, 0))
            pl.when(meta[0] != 0)(partial(send, 1))
            moves = [
                pltpu.make_async_copy(k.places[7].at[0:RW, :], by_narrow.at[0], sems.at[5])
            ]
            moves[0].start()
            moves += [output(0, i) for i in range(2)]
            for q, (buffer, out, (first, height, columns)) in enumerate(
                zip((wide, lift, down), (by_wide, by_lift, by_down), big_places())
            ):
                for c in range(columns):
                    part = give[first + c * height : first + (c + 1) * height, :]
                    buffer[:, c * LANES : (c + 1) * LANES] = part.astype(F32)
                width = columns * LANES
                at = pl.multiple_of((1 - meta[0]) * width, LANES)
                moves.append(
                    pltpu.make_async_copy(buffer, out.at[0, :, pl.ds(at, width)], sems.at[q])
                )
                moves[-1].start()
            lower = meta[0] == 0
            own, other = keep[AT_V:, :], give[AT_V:, :].astype(F32)
            rows[0:16, :] = jnp.where(lower, own, other)
            rows[16:, :] = jnp.where(lower, other, own)
            at = 0
            for columns, out in ((CW, wide_b), (CW, lift_b), (CD, down_b)):
                whole = [rows[h + at + i : h + at + i + 1, :] for h in (0, 16) for i in range(columns)]
                pick(meta, jnp.concatenate(whole, axis=1), out)
                at += columns
            rows[0:16, :] = late[RW + 3 * N :, :]
            chunk(meta, rows, 0, 1, narrow_b)
            chunk(meta, rows, 1, 1, by_skip)
            chunk(meta, rows, 8, DC // LANES, gain)
            chunk(meta, rows, 8 + DC // LANES, DC // LANES, shift)
            per = HC // nd
            for i in range(3):
                turned[...] = jnp.transpose(late[RW + i * N : RW + (i + 1) * N, :])
                by_ssm[i][0] = turned[pl.ds(pl.multiple_of(meta[2] * per, per), per), :]
            for move in moves:
                move.wait()

        return kernels[0](
            "finish",
            body,
            [
                *((part.shape, F32) for part in own),
                ((1, FW // nd), F32),
                ((1, FW // nd), F32),
                ((1, D // nd), F32),
                ((1, RW, HC), F32),
                ((1, HC // nd), F32),
                ((1, HC // nd, N), F32),
                ((1, HC // nd, N), F32),
                ((1, HC // nd, N), F32),
                ((1, HC // nd), F32),
                ((1, DC // nd), F32),
                ((1, DC // nd), F32),
                ((1, 2, T, DC), F32),
            ],
            vin=(*big, small),
            places=(*own, *lower, *upper, small),
            direct=(0, 1, 2, 6, 14),
            onto=3,
            scratch=[
                pltpu.VMEM((RW, HALVES[0]), F32),
                pltpu.VMEM((RL, HALVES[1]), F32),
                pltpu.VMEM((RD, HALVES[2]), F32),
                pltpu.VMEM((32, LANES), F32),
                pltpu.VMEM((HC, N), F32),
                pltpu.SemaphoreType.DMA((6,)),
            ],
        )

    xhat0, rstd0 = norm0(after=())
    normed0, narrow_pre0, act0, final0, pack0, pack1, narrow_w0 = front(
        0, xhat0, (pack, pack_other), narrow_w
    )
    arrived = line(final0)
    wide_pre0, wide_w0 = wide0(normed0, pack0)
    enter0, scanned0 = carry(0, act0, arrived, pack0, after=(wide_pre0,))
    pieces = gather(scanned0)
    lift_w0, down_w0 = choose(0, (lift_w, down_w), after=(scanned0,))
    scanned_all0, lifted0, gated0, *sends = middle0(pieces, wide_pre0, pack0, lift_w0, down_w0)
    parts = scatter(sends)
    narrow_w1, wide_w1, lift_w1, down_w1 = choose(
        1, (narrow_w, wide_w, lift_w, down_w), after=(sends[0],)
    )
    d_gated1, out_low1 = grad_gated1(down_w1, after=(sends[0],))
    hidden, hidden_low = layer_output(0, layer_input, parts, pack0, after=(d_gated1,))
    pieces = gather(hidden_low, forward=True)
    lefts0 = turn(0, (normed0, scanned_all0, gated0), after=(hidden_low,))
    lefts0_other, hidden_other = swap(lefts0), swap(hidden)

    normed1, narrow_pre1, act1, final1, xhat1, rstd1 = front(
        1, pieces, pack1, narrow_w1, after=(lefts0,)
    )
    wide_pre1, lift_low1, *sends = wide1(normed1, d_gated1, pack1, wide_w1, lift_w1, after=(final1,))
    arrived = line(final1)
    parts = scatter(sends)
    enter1, scanned1 = carry(1, act1, arrived, pack1, after=(sends[0],))
    pieces = gather(scanned1)
    d_scanned1, first1 = adjoint_local(1, parts, pack1, after=(scanned1, lefts0_other, hidden_other))
    scanned_all1, gated1, wide_low1 = middle1(pieces, wide_pre1, d_gated1, pack1, lift_w1)
    arrived = line(first1)
    states1 = states_before(1, act1, enter1, pack1, after=(wide_low1,))
    incoming1, narrow_low1 = adjoint(1, d_scanned1, narrow_pre1, arrived, pack1, after=(states1,))
    sends = grad_normed(1, wide_low1, narrow_low1, xhat1, pack1, wide_w1, narrow_w1)
    parts = scatter(sends)
    lefts1 = turn(1, (normed1, scanned_all1, gated1), after=(sends[0],))
    rights1, rights1_give = halve(1, (wide_low1, lift_low1, out_low1), after=(lefts1,))
    lefts1_other, rights1_other = swap(lefts1), swap(rights1_give)
    (late1,) = ssm_grads(
        1,
        act1,
        states1,
        d_scanned1,
        incoming1,
        lefts1,
        narrow_low1,
        pack1,
        (),
        after=(rights1,),
    )
    grad_mid, grad_low = layer_grad(1, parts, rstd1, xhat1, out_cotangent, pack1, after=(late1,))
    pieces = gather(grad_low)
    weights1 = weight_grads(
        1, (lefts1, lefts1_other), (rights1, rights1_other), after=(grad_low,)
    )
    big1 = to_pairs(weights1, 0)

    top_keep, top_give = top_parts(gated1, down_w1, after=(weights1[0],))
    top_arrived = paired(top_give, "tensor", 1)

    wide_low0, lift_low0, out_low0, *sends = grad_middle0(
        pieces, wide_pre0, lifted0, down_w0, lift_w0, after=(weights1[0], top_keep)
    )
    parts = scatter(sends)
    rights0, rights0_give = halve(0, (wide_low0, lift_low0, out_low0), after=())
    rights0_other = swap(rights0_give)
    for step in range(1, STEPS):
        weights1 = blocks_join(1, weights1, big1, (rights0,))
        big1 = to_pairs(weights1, step)
    d_scanned0, first0 = adjoint_local(0, parts, pack0, after=(rights0, weights1[0]))
    arrived = line(first0)
    weights0 = weight_grads(
        0, (lefts0, lefts0_other), (rights0, rights0_other), after=(first0,)
    )
    big0 = to_pairs(weights0, 0)
    incoming0, narrow_low0 = adjoint(
        0, d_scanned0, narrow_pre0, arrived, pack0, after=(weights0[0], *big1)
    )
    sends = grad_normed(
        0, wide_low0, narrow_low0, xhat0, pack0, wide_w0, narrow_w0
    )
    parts = scatter(sends)
    states0 = states_before(0, act0, enter0, pack0, after=(sends[0],))
    (sum1,) = big_sum(1, weights1, big1, (), after=(sends[0],))
    top = paired_sum(1, top_keep, top_give, top_arrived, (hidden, pack1), (sends[0],))
    for step in range(1, STEPS):
        weights0 = blocks_join(0, weights0, big0, (sum1, top[0], states0))
        big0 = to_pairs(weights0, step)
    late, late_give = ssm_grads(
        0,
        act0,
        states0,
        d_scanned0,
        incoming0,
        lefts0,
        narrow_low0,
        pack0,
        (late1,),
        after=(weights0[0],),
    )
    grad, grad_give = layer_grad(
        0, parts, rstd0, xhat0, grad_mid, pack0, after=(late, sum1, top[0])
    )
    grad_other = swap(grad_give)
    small_parts = late_join(late, swap(late_give), grad, grad_other, after=())
    small_parts_in = scatter(small_parts, "dp")
    keep, give = big_sum(0, weights0, big0, (sum1,), after=(small_parts[0],))
    big_other = swap(give)
    *own, input_grad, token = own_columns(keep, grad, grad_other, after=())
    (output,) = layer_output(1, None, top, pack1, after=(token,))
    (
        by_wide,
        by_lift,
        by_down,
        wide_b,
        lift_b,
        down_b,
        by_narrow,
        narrow_b,
        by_decay,
        by_input,
        by_output,
        by_skip,
        gain,
        shift,
        section_output,
    ) = finish(
        own,
        (keep, big_other),
        late_sum(small_parts_in),
        (hidden, hidden_other),
        (output, swap(output)),
    )
    return (
        section_output,
        input_grad,
        gain,
        shift,
        by_wide,
        wide_b,
        by_narrow,
        narrow_b,
        by_decay,
        by_input,
        by_output,
        by_skip,
        by_lift,
        lift_b,
        by_down,
        down_b,
    )


def solution(mesh):
    placed = (
        P(None, "dp", None),
        P(None, "dp", None),
        P(),
        P("section", None),
        P("section", None),
        P("section", None, "tensor"),
        P("section", "tensor"),
        P("section", None, "tensor"),
        P("section", "tensor"),
        P("section", "tensor", None),
        P("section", "tensor", None),
        P("section", "tensor", None),
        P("section", "tensor"),
        P("section", None, "tensor"),
        P("section", "tensor"),
        P("section", "tensor", None),
        P("section", None),
    )
    return jax.shard_map(
        local,
        mesh=mesh,
        in_specs=placed,
        out_specs=(
            P("section", None, "dp", "tensor"),
            P("section", None, "dp", "tensor"),
            P("section", ("tensor", "dp")),
            P("section", ("tensor", "dp")),
            P("section", "dp", "tensor"),
            P("section", ("tensor", "dp")),
            P("section", "dp", "tensor"),
            P("section", ("tensor", "dp")),
            P("section", ("tensor", "dp"), None),
            P("section", ("tensor", "dp"), None),
            P("section", ("tensor", "dp"), None),
            P("section", ("tensor", "dp")),
            P("section", "dp", "tensor"),
            P("section", ("tensor", "dp")),
            P("section", ("tensor", "dp"), None),
            P("section", "dp"),
        ),
        check_vma=False,
    )
```
